256 devices in a mesh: dp: 64 (over x, z, y_hi), seq: 4 (over y_lo, core).
Axes of the slice: x: 4, y: 4 (y_hi: 2, y_lo: 2; y = y_hi * 2 + y_lo), z: 8, core: 2. Of those that a mesh axis runs over, the one named last changes fastest.
Arguments:
- stash: bfloat16 [1024, 8192], P('dp', 'seq'), may hold values from -6 to 6
- grad_out: bfloat16 [1024, 8192], P('dp', 'seq'), may hold values from -1.5 to 1.5
- gate_weight: bfloat16 [14336, 8192], P('dp', 'seq'), may hold values from -0.0625 to 0.0625
- up_weight: bfloat16 [14336, 8192], P('dp', 'seq'), may hold values from -0.0625 to 0.0625
- down_weight: bfloat16 [14336, 8192], P('dp', 'seq'), may hold values from -0.046875 to 0.046875
Outputs:
- grad_input: bfloat16 [1024, 8192], P('dp', 'seq')
- grad_gate: float32 [14336, 8192], P('dp', 'seq')
- grad_up: float32 [14336, 8192], P('dp', 'seq')
- grad_down: float32 [14336, 8192], P('dp', 'seq')
The draws below stay inside these ranges and needn't reach their ends.
All inputs are finite; a program needn't handle non-finite values.
Results may differ from the reference program's by a relative error of at most 0.0049.
Values may be sent and summed in bfloat16 or wider, within the bound.
No kernel may reach another device: no remote copies, remote signals or barrier semaphores. Data moves between devices by JAX's collectives and lax.ppermute only.
A program may use at most 128 MiB of HBM per device.

```python
import jax
import jax.numpy as jnp

D = 8192
FF = 14336
TOK_BLK = 16
TOKENS = 1024


def level_of(stream_key, dims, shards, smallest, high):
    gain, own = 1.0, jax.random.fold_in(stream_key, 6)
    for position, parts in shards:
        steps = jnp.exp(jax.random.uniform(jax.random.fold_in(own, position), (parts,), jnp.float32, smallest / len(shards), high / len(shards)))
        gain = gain * jnp.repeat(steps, dims[position] // parts).reshape([-1 if axis == position else 1 for axis in range(len(dims))])
    return gain


def scatter_about(key, extent, scale, most, pieces=(), kind=jnp.bfloat16):
    factor_of = level_of(key, extent, pieces, -0.22, 0.18) if pieces else 1.0
    entries = jax.random.normal(key, extent, jnp.float32) * scale * factor_of
    return jnp.minimum(jnp.maximum(entries, -most), most).astype(kind)


def setup_inputs(seed: int = 0) -> dict:
    splits = jax.random.split(jax.random.key(seed), 6)
    stash = scatter_about(splits[0], (TOKENS, D), 1.0, 6.0, ((0, 64), (1, 4)))
    grad_out = scatter_about(splits[1], (TOKENS, D), 0.25, 1.5, ((0, 64), (1, 4)))
    gate_weight = scatter_about(splits[2], (FF, D), D ** -0.5, 0.0625, ((0, 64), (1, 4)))
    up_weight = scatter_about(splits[3], (FF, D), D ** -0.5, 0.0625, ((0, 64), (1, 4)))
    down_weight = scatter_about(splits[4], (FF, D), FF ** -0.5, 0.046875, ((0, 64), (1, 4)))
    return {"stash": stash, "grad_out": grad_out, "gate_weight": gate_weight, "up_weight": up_weight, "down_weight": down_weight}


def swiglu_back(gate, up, grad_hidden):
    sig = jax.nn.sigmoid(gate)
    act = gate * sig
    hidden = (act * up).astype(jnp.bfloat16)
    grad_gate_act = (grad_hidden * up * sig * (1.0 + gate * (1.0 - sig))).astype(jnp.bfloat16)
    grad_up_act = (grad_hidden * act).astype(jnp.bfloat16)
    return hidden, grad_gate_act, grad_up_act


def reference(stash, grad_out, gate_weight, up_weight, down_weight):
    inputs = jnp.roll(stash, TOK_BLK, axis=0)
    gate = jnp.dot(inputs, gate_weight.T, preferred_element_type=jnp.float32)
    up = jnp.dot(inputs, up_weight.T, preferred_element_type=jnp.float32)
    grad_hidden = jnp.dot(grad_out, down_weight.T, preferred_element_type=jnp.float32)
    hidden, grad_gate_act, grad_up_act = swiglu_back(gate, up, grad_hidden)
    grad_down = jnp.dot(hidden.T, grad_out, preferred_element_type=jnp.float32)
    grad_gate = jnp.dot(grad_gate_act.T, inputs, preferred_element_type=jnp.float32)
    grad_up = jnp.dot(grad_up_act.T, inputs, preferred_element_type=jnp.float32)
    grad_input = jnp.dot(grad_gate_act, gate_weight, preferred_element_type=jnp.float32)
    grad_input = grad_input + jnp.dot(grad_up_act, up_weight, preferred_element_type=jnp.float32)
    return grad_input.astype(jnp.bfloat16), grad_gate, grad_up, grad_down
```

```python
import jax
import jax.numpy as jnp
from jax import lax
from jax.sharding import PartitionSpec as P

NX, NZ, NH = 4, 8, 2
BF, F32 = jnp.bfloat16, jnp.float32


def dp_index(x, z, h):
    return ((x % NX) * NZ + z % NZ) * NH + h % NH


def hop(block, dx=0, dz=0, dh=0):
    route = [
        (dp_index(x, z, h), dp_index(x + dx, z + dz, h + dh))
        for x in range(NX)
        for z in range(NZ)
        for h in range(NH)
    ]
    return lax.ppermute(block, "dp", route)


def swap_core(block):
    return lax.ppermute(block, "seq", [(0, 1), (1, 0), (2, 3), (3, 2)])


def swap_chip(block):
    return lax.ppermute(block, "seq", [(0, 2), (2, 0), (1, 3), (3, 1)])


def dot_t(left, right):
    return lax.dot_general(left, right, (((1,), (1,)), ((), ())), preferred_element_type=F32)


def dot_first(left, right):
    return lax.dot_general(left, right, (((0,), (0,)), ((), ())), preferred_element_type=F32)


def pair_blocks(stash, grad_out, odd):
    n = NX * NZ * NH
    shifted = lax.ppermute(stash, "dp", [(i, (i + 1) % n) for i in range(n)])
    skipped = lax.ppermute(stash, "dp", [(i, (i + 2) % n) for i in range(1, n, 2)])
    other = hop(grad_out, dh=1)
    inputs = jnp.concatenate([jnp.where(odd, skipped, shifted), jnp.where(odd, shifted, stash)])
    cotangent = jnp.concatenate([jnp.where(odd, other, grad_out), jnp.where(odd, grad_out, other)])
    return inputs, cotangent


def ring_z(block):
    half = block.shape[0] // 2
    up1, dn1 = hop(block, dz=1), hop(block, dz=-1)
    up2, dn2 = hop(up1, dz=1), hop(dn1, dz=-1)
    up3, dn3 = hop(up2, dz=1), hop(dn2, dz=-1)
    far = jnp.concatenate([hop(up3[:half], dz=1), hop(dn3[half:], dz=-1)])
    return [block, up1, dn1, up2, dn2, up3, dn3, far]


def ring_x(block):
    half = block.shape[0] // 2
    up1, dn1 = hop(block, dx=1), hop(block, dx=-1)
    far = jnp.concatenate([hop(up1[:half], dx=1), hop(dn1[half:], dx=-1)])
    return [block, up1, dn1, far]


Z_OFF = [0, -1, 1, -2, 2, -3, 3, 4]
X_OFF = [0, -1, 1, 2]


def seq_sum(keep, send):
    chip = keep + swap_core(send)
    return chip + swap_chip(chip.astype(BF)).astype(F32)


def swiglu_back(gate, up, grad_hidden):
    sig = jax.nn.sigmoid(gate)
    act = gate * sig
    hidden = (act * up).astype(BF)
    grad_gate_act = (grad_hidden * up * sig * (1.0 + gate * (1.0 - sig))).astype(BF)
    grad_up_act = (grad_hidden * act).astype(BF)
    return hidden, grad_gate_act, grad_up_act


def per_device(stash, grad_out, gate_weight, up_weight, down_weight):
    odd = lax.axis_index("dp") % 2 == 1
    core1 = lax.axis_index("seq") % 2 == 1
    ff, width = gate_weight.shape
    inputs, cotangent = pair_blocks(stash, grad_out, odd)
    weight = jnp.concatenate([gate_weight, up_weight])

    row = jnp.concatenate([inputs, hop(inputs, dx=1), hop(inputs, dx=-1), hop(inputs, dx=2)])
    in_z = ring_z(row)
    cot_x = ring_x(jnp.concatenate(ring_z(cotangent)))

    gu = []
    for block in in_z:
        part = dot_t(block, weight)
        lo, hi = part[:64], part[64:]
        gu.append(seq_sum(jnp.where(core1, hi, lo), jnp.where(core1, lo, hi)))
    gh_parts = [dot_t(block, down_weight) for block in cot_x]
    gh = []
    for i, j in ((0, 2), (1, 3)):
        lo, hi = gh_parts[i], gh_parts[j]
        gh.append(seq_sum(jnp.where(core1, hi, lo), jnp.where(core1, lo, hi)))
    gu = jnp.stack([g.reshape(2, 32, 2 * ff) for g in gu])
    gh = jnp.stack([g.reshape(NZ, 32, ff) for g in gh], axis=1)
    hidden, gga, gua = swiglu_back(gu[..., :ff], gu[..., ff:], gh)
    acts = jnp.concatenate([hidden, gga, gua], axis=-1)
    theirs = swap_core(acts)
    acts = jnp.concatenate([jnp.where(core1, theirs, acts), jnp.where(core1, acts, theirs)], axis=1)
    zx = acts[..., ff:].reshape(1024, 2 * ff)
    xz_all = acts.transpose(1, 0, 2, 3).reshape(1024, 3 * ff)
    hidden, xz = xz_all[:, :ff], xz_all[:, ff:]

    half = width // 2
    left = jnp.dot(zx, weight[:, :half], preferred_element_type=F32).astype(BF).reshape(NZ, 128, half)
    right = jnp.dot(xz, weight[:, half:], preferred_element_type=F32).astype(BF).reshape(NX, 256, half)
    recv = [hop(right[X_OFF.index(o)], dx=o) for o in (2, 1, -1)]
    part = {o: left[Z_OFF.index(o)] for o in Z_OFF}

    def add(a, b):
        return (a.astype(F32) + b.astype(F32)).astype(BF)

    up = hop(part[4][:64], dz=1)
    dn = hop(part[4][64:], dz=-1)
    up = jnp.concatenate([add(part[3][:64], up), part[3][64:]])
    dn = jnp.concatenate([part[-3][:64], add(part[-3][64:], dn)])
    up, dn = hop(up, dz=1), hop(dn, dz=-1)
    up, dn = hop(add(part[2], up), dz=1), hop(add(part[-2], dn), dz=-1)
    up, dn = hop(add(part[1], up), dz=1), hop(add(part[-1], dn), dz=-1)
    left = part[0].astype(F32) + up.astype(F32) + dn.astype(F32)
    left = left.astype(BF).reshape(NX, 32, half)
    lsum = left[0].astype(F32)
    for o in (2, 1, -1):
        lsum = lsum + hop(left[X_OFF.index(o)], dx=o).astype(F32)

    right = right[0].astype(F32) + recv[0].astype(F32) + recv[1].astype(F32) + recv[2].astype(F32)
    right = right.astype(BF).reshape(NZ, 32, half)
    rsum = right[0].astype(F32)
    for o in Z_OFF[:0:-1]:
        rsum = rsum + hop(right[Z_OFF.index(o)], dz=o).astype(F32)
    total = jnp.concatenate([lsum, rsum], axis=1)
    mine = jnp.where(odd, total[16:], total[:16])
    sent = jnp.where(odd, total[:16], total[16:])
    grad_input = mine + hop(sent.astype(BF), dh=1).astype(F32)

    in_all = jnp.concatenate(in_z)
    cot_all = jnp.concatenate(cot_x)
    grad_gate = dot_first(zx[:, :ff], in_all)
    grad_up = dot_first(zx[:, ff:], in_all)
    grad_down = dot_first(hidden, cot_all)
    return grad_input.astype(BF), grad_gate, grad_up, grad_down


def solution(mesh):
    spec = P("dp", "seq")
    return jax.shard_map(
        per_device, mesh=mesh, in_specs=(spec,) * 5, out_specs=(spec,) * 4, check_vma=False
    )
```

```python
import functools

import jax
import jax.numpy as jnp
from jax import lax
from jax.experimental import pallas as pl
from jax.experimental.pallas import tpu as pltpu
from jax.sharding import PartitionSpec as P

NX, NZ, NH = 4, 8, 2
BF, F32 = jnp.bfloat16, jnp.float32
Z_OFF = (0, -1, 1, -2, 2, -3, 3, 4)
X_OFF = (0, -1, 1, 2)
GROUPS = ((0, 1, 2, 3, 4), (5, 6, 7))
TOK = 16
FF = 256
LIMIT = 32 * 2**20


def dp_index(x, z, h):
    return ((x % NX) * NZ + z % NZ) * NH + h % NH


def hop(block, dx=0, dz=0, dh=0):
    route = [
        (dp_index(x, z, h), dp_index(x + dx, z + dz, h + dh))
        for x in range(NX)
        for z in range(NZ)
        for h in range(NH)
    ]
    return lax.ppermute(block, "dp", route)


def swap_core(block):
    return lax.ppermute(block, "seq", [(0, 1), (1, 0), (2, 3), (3, 2)])


def swap_chip(block):
    return lax.ppermute(block, "seq", [(0, 2), (2, 0), (1, 3), (3, 1)])


def dot_t(left, right):
    return lax.dot_general(left, right, (((1,), (1,)), ((), ())), preferred_element_type=F32)


def dot_first(left, right):
    return lax.dot_general(left, right, (((0,), (0,)), ((), ())), preferred_element_type=F32)


def local(body, outs, *args, flag=None):
    specs = [pl.BlockSpec(memory_space=pltpu.VMEM)] * len(args)
    if flag is not None:
        specs = [pl.BlockSpec(memory_space=pltpu.SMEM)] + specs
        args = (flag,) + args
    size = sum(a.size * a.dtype.itemsize for a in args) + sum(
        o.size * jnp.dtype(o.dtype).itemsize for o in outs
    )
    return pl.pallas_call(
        body,
        out_shape=list(outs),
        in_specs=specs,
        out_specs=[pl.BlockSpec(memory_space=pltpu.VMEM)] * len(outs),
        compiler_params=pltpu.CompilerParams(vmem_limit_bytes=LIMIT),
        cost_estimate=pl.CostEstimate(flops=0, bytes_accessed=size, transcendentals=0),
    )(*args)


def shape(rows, cols, kind):
    return jax.ShapeDtypeStruct((rows, cols), kind)


def stack_body(*refs):
    out, at = refs[-1], 0
    for ref in refs[:-1]:
        rows = ref.shape[0]
        out[at : at + rows] = ref[...]
        at += rows


def stack(*blocks):
    rows = sum(b.shape[0] for b in blocks)
    return local(stack_body, [shape(rows, blocks[0].shape[1], blocks[0].dtype)], *blocks)[0]


def split_body(rows_in, flag, *refs):
    n = len(rows_in)
    gus, ghs, (keep, send) = refs[:n], refs[n:-2], refs[-2:]
    first = flag[0] == 0
    at = 0
    for ref, rows in zip(gus, rows_in):
        for i in range(rows // (2 * TOK)):
            a = ref[2 * TOK * i : 2 * TOK * i + TOK]
            b = ref[2 * TOK * i + TOK : 2 * TOK * (i + 1)]
            keep[at : at + TOK, : 2 * FF] = jnp.where(first, a, b)
            send[at : at + TOK, : 2 * FF] = jnp.where(first, b, a)
            at += TOK
    for x, ref in enumerate(ghs):
        for i in range(ref.shape[0] // (2 * TOK)):
            a = ref[2 * TOK * i : 2 * TOK * i + TOK]
            b = ref[2 * TOK * i + TOK : 2 * TOK * (i + 1)]
            at = (i * NX + x) * TOK
            keep[at : at + TOK, 2 * FF :] = jnp.where(first, a, b)
            send[at : at + TOK, 2 * FF :] = jnp.where(first, b, a)


def add_body(a, b, full, low):
    total = a[...] + b[...]
    full[...] = total
    low[...] = total.astype(BF)


def act_body(a, b, out):
    gate = a[:, :FF] + b[:, :FF].astype(F32)
    up = a[:, FF : 2 * FF] + b[:, FF : 2 * FF].astype(F32)
    grad_hidden = a[:, 2 * FF :] + b[:, 2 * FF :].astype(F32)
    sig = 1.0 / (1.0 + jnp.exp(-gate))
    act = gate * sig
    out[:, :FF] = (act * up).astype(BF)
    out[:, FF : 2 * FF] = (grad_hidden * up * sig * (1.0 + gate * (1.0 - sig))).astype(BF)
    out[:, 2 * FF :] = (grad_hidden * act).astype(BF)


def order_body(nz, flag, mine, theirs, *outs):
    by_x, hid, by_z = outs[:NX], outs[NX : 2 * NX], outs[2 * NX :]
    first = flag[0] == 0
    for z in range(nz):
        for x in range(NX):
            at = (z * NX + x) * TOK
            a, b = mine[at : at + TOK], theirs[at : at + TOK]
            for h, val in enumerate((jnp.where(first, a, b), jnp.where(first, b, a))):
                to = (2 * z + h) * TOK
                hid[x][to : to + TOK] = val[:, :FF]
                by_x[x][to : to + TOK] = val[:, FF:]
                to = (2 * x + h) * TOK
                by_z[z][to : to + TOK] = val[:, FF:]


def fold_body(own, a, b, c, *outs):
    for i, out in enumerate(outs):
        s = slice(2 * TOK * i, 2 * TOK * (i + 1))
        total = own[s] + a[s].astype(F32) + b[s].astype(F32) + c[s].astype(F32)
        out[...] = total.astype(out.dtype)


def last_body(own, *refs):
    parts, (mine, other) = refs[:-2], refs[-2:]
    total = own[...]
    for part in parts:
        total = total + part[...].astype(F32)
    mine[...] = total[:TOK]
    other[...] = total[TOK:]


def weight_grad_body(n, lo, *refs):
    acts, blocks, out = refs[:n], refs[n : 2 * n], refs[-1]
    left = jnp.concatenate([a[:, lo : lo + FF] for a in acts])
    right = jnp.concatenate([b[...] for b in blocks])
    out[...] = dot_first(left, right)[: out.shape[0]]


def weight_grad(acts, blocks, lo, ff):
    width, tile = blocks[0].shape[1], 512
    rows = sum(b.shape[0] for b in blocks)
    return pl.pallas_call(
        functools.partial(weight_grad_body, len(acts), lo),
        grid=(width // tile,),
        in_specs=[pl.BlockSpec(a.shape, lambda j: (0, 0)) for a in acts]
        + [pl.BlockSpec((b.shape[0], tile), lambda j: (0, j)) for b in blocks],
        out_specs=pl.BlockSpec((ff, tile), lambda j: (0, j)),
        out_shape=shape(ff, width, F32),
        compiler_params=pltpu.CompilerParams(vmem_limit_bytes=LIMIT),
        cost_estimate=pl.CostEstimate(
            flops=2 * rows * FF * width, bytes_accessed=2 * rows * width + 4 * ff * width, transcendentals=0
        ),
    )(*acts, *blocks)


def per_device(stash, grad_out, gate_weight, up_weight, down_weight):
    core = (lax.axis_index("seq") % 2).astype(jnp.int32).reshape(1)
    ff, width = gate_weight.shape
    n = NX * NZ * NH
    own = lax.ppermute(stash, "dp", [(i, (i + 1) % n) for i in range(n)])
    other = lax.ppermute(stash, "dp", [(i, (i + 2 * (i % 2)) % n) for i in range(n)])
    cot_other = hop(grad_out, dh=1)
    pad = jnp.zeros((FF - ff, width), BF)
    weight = jnp.concatenate([gate_weight, pad, up_weight, pad])
    down = jnp.concatenate([down_weight, pad])

    cot = stack(grad_out, cot_other)
    pair = stack(own, other)
    cu1, cd1 = hop(cot, dz=1), hop(cot, dz=-1)
    row = stack(pair, hop(pair, dx=1), hop(pair, dx=-1), hop(pair, dx=2))
    cu2, cd2 = hop(cu1, dz=1), hop(cd1, dz=-1)
    u1, d1 = hop(row, dz=1), hop(row, dz=-1)
    near = stack(cot, cu1, cd1, cu2, cd2)
    cu3, cd3 = hop(cu2, dz=1), hop(cd2, dz=-1)
    near_u, near_d = hop(near, dx=1), hop(near, dx=-1)
    u2, d2 = hop(u1, dz=1), hop(d1, dz=-1)
    far = stack(cu3, cd3, hop(cd3, dz=-1))
    near_f = hop(near_u, dx=1)
    far_u, far_d = hop(far, dx=1), hop(far, dx=-1)
    u3, d3 = hop(u2, dz=1), hop(d2, dz=-1)
    far_f = hop(far_d, dx=-1)
    half = row.shape[0] // 2
    f_lo, f_hi = hop(u3[:half], dz=1), hop(d3[half:], dz=-1)
    in_z = [[row, u1, d1, u2, d2], [u3, d3, f_lo, f_hi]]
    cot_x = [[near, near_u, near_d, near_f], [far, far_u, far_d, far_f]]

    hiddens, by_zs, own_sum, sent = [], [], None, []
    for group in range(2):
        nz = len(GROUPS[group])
        gu = [dot_t(b, weight) for b in in_z[group]]
        gh = [dot_t(b, down) for b in cot_x[group]]
        tokens = nz * NX * TOK
        keep, send = local(
            functools.partial(split_body, [b.shape[0] for b in gu]),
            [shape(tokens, 3 * FF, F32)] * 2, *gu, *gh, flag=core,
        )
        chip, low = local(
            add_body, [shape(tokens, 3 * FF, F32), shape(tokens, 3 * FF, BF)], keep, swap_core(send)
        )
        acts = local(act_body, [shape(tokens, 3 * FF, BF)], chip, swap_chip(low))[0]
        ordered = local(
            functools.partial(order_body, nz),
            [shape(nz * 2 * TOK, 2 * FF, BF)] * NX
            + [shape(nz * 2 * TOK, FF, BF)] * NX
            + [shape(NX * 2 * TOK, 2 * FF, BF)] * nz,
            acts, swap_core(acts), flag=core,
        )
        by_x, hid, by_z = ordered[:NX], ordered[NX : 2 * NX], ordered[2 * NX :]
        hiddens += hid
        by_zs += by_z
        recv = [
            hop(jnp.dot(by_x[X_OFF.index(o)], weight, preferred_element_type=F32).astype(BF), dx=o)
            for o in (2, 1, -1)
        ]
        mine = jnp.dot(by_x[0], weight, preferred_element_type=F32)
        kinds = [F32 if Z_OFF[z] == 0 else BF for z in GROUPS[group]]
        folded = local(fold_body, [shape(2 * TOK, width, k) for k in kinds], mine, *recv)
        for z, block in zip(GROUPS[group], folded):
            if Z_OFF[z] == 0:
                own_sum = block
            else:
                sent.append(hop(block, dz=Z_OFF[z]))
    keep, give = local(last_body, [shape(TOK, width, F32)] * 2, own_sum, *sent)
    grad_input = (keep + hop(give, dh=1)).astype(BF)

    in_rows = in_z[0] + in_z[1][:2] + [stack(*in_z[1][2:])]
    grad_gate = weight_grad(by_zs, in_rows, 0, ff)
    grad_up = weight_grad(by_zs, in_rows, FF, ff)
    grad_down = weight_grad(hiddens, cot_x[0] + cot_x[1], 0, ff)
    return grad_input, grad_gate, grad_up, grad_down


def solution(mesh):
    spec = P("dp", "seq")
    return jax.shard_map(
        per_device, mesh=mesh, in_specs=(spec,) * 5, out_specs=(spec,) * 4, check_vma=False
    )
```

```python
import functools

import jax
import jax.numpy as jnp
from jax import lax
from jax.experimental import pallas as pl
from jax.experimental.pallas import tpu as pltpu
from jax.sharding import PartitionSpec as P

NX, NZ, NH = 4, 8, 2
BF, F32 = jnp.bfloat16, jnp.float32
Z_OFF = (0, -1, 1, -2, 2, -3, 3, 4)
X_OFF = (0, -1, 1, 2)
GROUPS = ((0, 1, 2, 3, 4), (5, 6, 7))
TOK = 16
FF = 256
LIMIT = 16 * 2**20
SMALL = pl.CostEstimate(flops=1, bytes_accessed=1, transcendentals=0)


def dp_index(x, z, h):
    return ((x % NX) * NZ + z % NZ) * NH + h % NH


def hop(block, dx=0, dz=0, dh=0):
    route = [
        (dp_index(x, z, h), dp_index(x + dx, z + dz, h + dh))
        for x in range(NX)
        for z in range(NZ)
        for h in range(NH)
    ]
    return lax.ppermute(block, "dp", route)


def swap_core(block):
    return lax.ppermute(block, "seq", [(0, 1), (1, 0), (2, 3), (3, 2)])


def swap_chip(block):
    return lax.ppermute(block, "seq", [(0, 2), (2, 0), (1, 3), (3, 1)])


def dot_t(left, right):
    return lax.dot_general(left, right, (((1,), (1,)), ((), ())), preferred_element_type=F32)


def dot_first(left, right):
    return lax.dot_general(left, right, (((0,), (0,)), ((), ())), preferred_element_type=F32)


def local(body, outs, *args, flag=None):
    specs = [pl.BlockSpec(memory_space=pltpu.VMEM)] * len(args)
    if flag is not None:
        specs = [pl.BlockSpec(memory_space=pltpu.SMEM)] + specs
        args = (flag,) + args
    return pl.pallas_call(
        body,
        out_shape=list(outs),
        in_specs=specs,
        out_specs=[pl.BlockSpec(memory_space=pltpu.VMEM)] * len(outs),
        compiler_params=pltpu.CompilerParams(vmem_limit_bytes=LIMIT),
        cost_estimate=SMALL,
    )(*args)


def shape(rows, cols, kind):
    return jax.ShapeDtypeStruct((rows, cols), kind)


def stack_body(*refs):
    out, at = refs[-1], 0
    for ref in refs[:-1]:
        rows = ref.shape[0]
        out[at : at + rows] = ref[...]
        at += rows


def stack(*blocks):
    rows = sum(b.shape[0] for b in blocks)
    return local(stack_body, [shape(rows, blocks[0].shape[1], blocks[0].dtype)], *blocks)[0]


def split_body(rows_in, flag, *refs):
    n = len(rows_in)
    gus, ghs, (keep, send) = refs[:n], refs[n:-2], refs[-2:]
    first = flag[0] == 0
    at = 0
    for ref, rows in zip(gus, rows_in):
        for i in range(rows // (2 * TOK)):
            a = ref[2 * TOK * i : 2 * TOK * i + TOK]
            b = ref[2 * TOK * i + TOK : 2 * TOK * (i + 1)]
            keep[at : at + TOK, : 2 * FF] = jnp.where(first, a, b)
            send[at : at + TOK, : 2 * FF] = jnp.where(first, b, a)
            at += TOK
    for x, ref in enumerate(ghs):
        for i in range(ref.shape[0] // (2 * TOK)):
            a = ref[2 * TOK * i : 2 * TOK * i + TOK]
            b = ref[2 * TOK * i + TOK : 2 * TOK * (i + 1)]
            at = (i * NX + x) * TOK
            keep[at : at + TOK, 2 * FF :] = jnp.where(first, a, b)
            send[at : at + TOK, 2 * FF :] = jnp.where(first, b, a)


def add_body(a, b, full, low):
    total = a[...] + b[...]
    full[...] = total
    low[...] = total.astype(BF)


def act_body(a, b, out):
    gate = a[:, :FF] + b[:, :FF].astype(F32)
    up = a[:, FF : 2 * FF] + b[:, FF : 2 * FF].astype(F32)
    grad_hidden = a[:, 2 * FF :] + b[:, 2 * FF :].astype(F32)
    sig = 1.0 / (1.0 + jnp.exp(-gate))
    act = gate * sig
    out[:, :FF] = (act * up).astype(BF)
    out[:, FF : 2 * FF] = (grad_hidden * up * sig * (1.0 + gate * (1.0 - sig))).astype(BF)
    out[:, 2 * FF :] = (grad_hidden * act).astype(BF)


def order_body(nz, flag, mine, theirs, *outs):
    by_x, hid, by_z = outs[:NX], outs[NX : 2 * NX], outs[2 * NX :]
    first = flag[0] == 0
    for z in range(nz):
        for x in range(NX):
            at = (z * NX + x) * TOK
            a, b = mine[at : at + TOK], theirs[at : at + TOK]
            for h, val in enumerate((jnp.where(first, a, b), jnp.where(first, b, a))):
                to = (2 * z + h) * TOK
                hid[x][to : to + TOK] = val[:, :FF]
                by_x[x][to : to + TOK] = val[:, FF:]
                to = (2 * x + h) * TOK
                by_z[z][to : to + TOK] = val[:, FF:]


def fold_body(own, a, b, c, keep, send):
    for i in range(keep.shape[0] // TOK):
        for h, out in enumerate((keep, send)):
            s = slice((2 * i + h) * TOK, (2 * i + h + 1) * TOK)
            total = own[s] + a[s].astype(F32) + b[s].astype(F32) + c[s].astype(F32)
            out[i * TOK : (i + 1) * TOK] = total.astype(out.dtype)


def join_body(keep, recv, *outs):
    for i, out in enumerate(outs):
        s = slice(i * TOK, (i + 1) * TOK)
        out[...] = (keep[s] + recv[s].astype(F32)).astype(out.dtype)


def last_body(own, *refs):
    parts, out = refs[:-1], refs[-1]
    total = own[...]
    for part in parts:
        total = total + part[...].astype(F32)
    out[...] = total.astype(BF)


def weight_grad_body(n, lo, *refs):
    acts, blocks, out = refs[:n], refs[n : 2 * n], refs[-1]
    left = jnp.concatenate([a[:, lo : lo + FF] for a in acts])
    right = jnp.concatenate([b[...] for b in blocks])
    out[...] = dot_first(left, right)[: out.shape[0]]


def weight_grad(acts, blocks, lo, ff):
    width, tile = blocks[0].shape[1], 512
    return pl.pallas_call(
        functools.partial(weight_grad_body, len(acts), lo),
        grid=(width // tile,),
        in_specs=[pl.BlockSpec(a.shape, lambda j: (0, 0)) for a in acts]
        + [pl.BlockSpec((b.shape[0], tile), lambda j: (0, j)) for b in blocks],
        out_specs=pl.BlockSpec((ff, tile), lambda j: (0, j)),
        out_shape=shape(ff, width, F32),
        compiler_params=pltpu.CompilerParams(vmem_limit_bytes=LIMIT),
        cost_estimate=SMALL,
    )(*acts, *blocks)


def tie_body(*refs):
    pass


def tie(values, *after):
    n = len(values)
    return pl.pallas_call(
        tie_body,
        out_shape=[jax.ShapeDtypeStruct(v.shape, v.dtype) for v in values],
        in_specs=[pl.BlockSpec(memory_space=pl.ANY)] * (n + len(after)),
        out_specs=[pl.BlockSpec(memory_space=pl.ANY)] * n,
        input_output_aliases={i: i for i in range(n)},
        compiler_params=pltpu.CompilerParams(vmem_limit_bytes=2**20),
        cost_estimate=SMALL,
    )(*values, *after)


def pack_body(gate, up, down, weight, down_out):
    ff, width = gate.shape
    pad = jnp.zeros((FF - ff, width), BF)
    weight[:ff] = gate[...]
    weight[ff:FF] = pad
    weight[FF : FF + ff] = up[...]
    weight[FF + ff :] = pad
    down_out[:ff] = down[...]
    down_out[ff:] = pad


def pair_body(own, other, cot_own, cot_other, pair, cot):
    pair[:TOK] = own[...]
    pair[TOK:] = other[...]
    cot[:TOK] = cot_own[...]
    cot[TOK:] = cot_other[...]


def gather_body(pair, x1, x2, x3, cot, u1, d1, u2, d2, weight, down, row, near):
    for i, ref in enumerate((pair, x1, x2, x3)):
        row[2 * TOK * i : 2 * TOK * (i + 1)] = ref[...]
    for i, ref in enumerate((cot, u1, d1, u2, d2)):
        near[2 * TOK * i : 2 * TOK * (i + 1)] = ref[...]


def back_body(b0, b1, b2, b3, weight, o1, o2, o3, own):
    @pl.loop(0, weight.shape[1] // 512)
    def _(j):
        cols = pl.ds(pl.multiple_of(j * 512, 512), 512)
        for block, out in ((b3, o3), (b1, o1), (b2, o2), (b0, own)):
            part = jnp.dot(block[...], weight[:, cols], preferred_element_type=F32)
            out[:, cols] = part.astype(out.dtype)


def per_device(stash, grad_out, gate_weight, up_weight, down_weight):
    core = (lax.axis_index("seq") % 2).astype(jnp.int32).reshape(1)
    ff, width = gate_weight.shape
    n = NX * NZ * NH
    own = lax.ppermute(stash, "dp", [(i, (i + 1) % n) for i in range(n)])
    other = lax.ppermute(stash, "dp", [(i, (i + 2 * (i % 2)) % n) for i in range(n)])
    cot_other = hop(grad_out, dh=1)
    weight, down = local(
        pack_body, [shape(2 * FF, width, BF), shape(FF, width, BF)], gate_weight, up_weight, down_weight
    )

    pair, cot = local(pair_body, [shape(2 * TOK, width, BF)] * 2, own, other, grad_out, cot_other)
    x1, x2, x3 = hop(pair, dx=1), hop(pair, dx=-1), hop(pair, dx=2)
    cu1, cd1, cu2, cd2 = [hop(cot, dz=o) for o in (1, -1, 2, -2)]
    row, near = pl.pallas_call(
        gather_body,
        out_shape=[shape(8 * TOK, width, BF), shape(10 * TOK, width, BF)],
        in_specs=[pl.BlockSpec(memory_space=pltpu.VMEM)] * 9 + [pl.BlockSpec(memory_space=pl.ANY)] * 2,
        out_specs=[pl.BlockSpec(memory_space=pltpu.VMEM)] * 2,
        compiler_params=pltpu.CompilerParams(vmem_limit_bytes=LIMIT),
        cost_estimate=SMALL,
    )(pair, x1, x2, x3, cot, cu1, cd1, cu2, cd2, weight, down)
    u1, d1 = hop(row, dz=1), hop(row, dz=-1)
    near_u, near_d = hop(near, dx=1), hop(near, dx=-1)
    cu3, cd3 = hop(cu2, dz=1), hop(cd2, dz=-1)
    u1, d1, near_u, near_d, cu3, cd3 = tie([u1, d1, near_u, near_d, cu3, cd3])
    u2, d2 = hop(u1, dz=1), hop(d1, dz=-1)
    near_f, c4 = hop(near_u, dx=1), hop(cd3, dz=-1)
    u2, d2, near_f, c4 = tie([u2, d2, near_f, c4])
    far = stack(cu3, cd3, c4)
    u3, d3 = hop(u2, dz=1), hop(d2, dz=-1)
    far_u, far_d = hop(far, dx=1), hop(far, dx=-1)

    def halves(blocks, parts):
        gu = [dot_t(b, weight) for b in blocks]
        gh = [dot_t(b, down) for b in parts]
        tokens = sum(b.shape[0] for b in blocks) // 2
        return local(
            functools.partial(split_body, [b.shape[0] for b in gu]),
            [shape(tokens, 3 * FF, F32)] * 2, *gu, *gh, flag=core,
        )

    def chip_sum(keep, recv):
        return local(
            add_body, [shape(keep.shape[0], 3 * FF, F32), shape(keep.shape[0], 3 * FF, BF)], keep, recv
        )

    def acts_of(chip, recv):
        return local(act_body, [shape(chip.shape[0], 3 * FF, BF)], chip, recv)[0]

    def order(acts, theirs, nz):
        out = local(
            functools.partial(order_body, nz),
            [shape(nz * 2 * TOK, 2 * FF, BF)] * NX
            + [shape(nz * 2 * TOK, FF, BF)] * NX
            + [shape(NX * 2 * TOK, 2 * FF, BF)] * nz,
            acts, theirs, flag=core,
        )
        return out[:NX], out[NX : 2 * NX], out[2 * NX :]

    def project(by_x):
        rows = by_x[0].shape[0]
        *out, mine = local(
            back_body, [shape(rows, width, BF)] * 3 + [shape(rows, width, F32)], *by_x, weight
        )
        return mine, out

    def scatter_x(out):
        return [hop(out[i], dx=X_OFF[i + 1]) for i in (2, 0, 1)]

    def fold(mine, recv):
        rows = mine.shape[0] // 2
        return local(fold_body, [shape(rows, width, F32), shape(rows, width, BF)], mine, *recv)

    def scatter_z(group, keep, recv):
        kinds = [F32 if Z_OFF[z] == 0 else BF for z in GROUPS[group]]
        joined = local(join_body, [shape(TOK, width, k) for k in kinds], keep, recv)
        return [b if Z_OFF[z] == 0 else hop(b, dz=Z_OFF[z]) for z, b in zip(GROUPS[group], joined)]

    in1, cot1 = [row, u1, d1, u2, d2], [near, near_u, near_d, near_f]
    keep1, send1 = halves(in1, cot1)
    chip1, low1 = chip_sum(keep1, swap_core(send1))
    their1 = swap_chip(low1)
    u3, d3, far_u, far_d, their1 = tie([u3, d3, far_u, far_d, their1])
    half = row.shape[0] // 2
    f_lo, f_hi = hop(u3[:half], dz=1), hop(d3[half:], dz=-1)
    far_f = hop(far_d, dx=-1)
    acts1 = acts_of(chip1, their1)
    by_x1, hid1, by_z1 = order(acts1, swap_core(acts1), len(GROUPS[0]))
    mine1, out1 = project(by_x1)
    recv1 = scatter_x(out1)
    far_f, mine1 = tie([far_f, mine1])
    f_lo, f_hi = tie([f_lo, f_hi], far_f)
    in2, cot2 = [u3, d3, f_lo, f_hi], [far, far_u, far_d, far_f]
    keep2, send2 = halves(in2, cot2)
    chip2, low2 = chip_sum(keep2, swap_core(send2))
    acts2 = acts_of(chip2, swap_chip(low2))
    by_x2, hid2, by_z2 = order(acts2, swap_core(acts2), len(GROUPS[1]))
    mine2, out2 = project(by_x2)
    recv2 = scatter_x(out2)
    in_rows = in1 + in2[:2] + [stack(*in2[2:])]
    by_z2, hid2 = tie(by_z2, mine2), tie(hid2, mine2)
    grad_gate = weight_grad(by_z1 + by_z2, in_rows, 0, ff)
    grad_up = weight_grad(by_z1 + by_z2, in_rows, FF, ff)
    grad_down = weight_grad(hid1 + hid2, cot1 + cot2, 0, ff)
    recv1 = tie(recv1, grad_gate, grad_up, grad_down)
    keep1, send1 = fold(mine1, recv1)
    own_sum, *sent = scatter_z(0, keep1, hop(send1, dh=1))
    recv2 = tie(recv2, own_sum)
    keep2, send2 = fold(mine2, recv2)
    sent2 = scatter_z(1, keep2, hop(send2, dh=1))
    (grad_input,) = local(last_body, [shape(TOK, width, BF)], own_sum, *sent, *sent2)
    return grad_input, grad_gate, grad_up, grad_down


def solution(mesh):
    spec = P("dp", "seq")
    return jax.shard_map(
        per_device, mesh=mesh, in_specs=(spec,) * 5, out_specs=(spec,) * 4, check_vma=False
    )
```

```python
import functools

import jax
import jax.numpy as jnp
from jax import lax
from jax.experimental import pallas as pl
from jax.experimental.pallas import tpu as pltpu
from jax.sharding import PartitionSpec as P

NX, NZ, NH = 4, 8, 2
BF, F32 = jnp.bfloat16, jnp.float32
Z_OFF = (0, -1, 1, -2, 2, -3, 3, 4)
X_OFF = (0, -1, 1, 2)
GROUPS = ((0, 1, 2, 3, 4), (5, 6, 7))
TOK = 16
FF = 256
LIMIT = 16 * 2**20
SMALL = pl.CostEstimate(flops=1, bytes_accessed=1, transcendentals=0)


def dp_index(x, z, h):
    return ((x % NX) * NZ + z % NZ) * NH + h % NH


def hop(block, dx=0, dz=0, dh=0):
    route = [
        (dp_index(x, z, h), dp_index(x + dx, z + dz, h + dh))
        for x in range(NX)
        for z in range(NZ)
        for h in range(NH)
    ]
    return lax.ppermute(block, "dp", route)


def swap_core(block):
    return lax.ppermute(block, "seq", [(0, 1), (1, 0), (2, 3), (3, 2)])


def swap_chip(block):
    return lax.ppermute(block, "seq", [(0, 2), (2, 0), (1, 3), (3, 1)])


def dot_t(left, right):
    return lax.dot_general(left, right, (((1,), (1,)), ((), ())), preferred_element_type=F32)


def dot_first(left, right):
    return lax.dot_general(left, right, (((0,), (0,)), ((), ())), preferred_element_type=F32)


def local(body, outs, *args, flag=None, after=()):
    n, first = len(args), 0 if flag is None else 1

    def run(*refs):
        body(*refs[: n + first], *refs[n + first + len(after) :])

    vmem, free = pl.BlockSpec(memory_space=pltpu.VMEM), pl.BlockSpec(memory_space=pl.ANY)
    return pl.pallas_call(
        run,
        out_shape=list(outs),
        in_specs=[pl.BlockSpec(memory_space=pltpu.SMEM)] * first + [vmem] * n + [free] * len(after),
        out_specs=[vmem] * len(outs),
        compiler_params=pltpu.CompilerParams(vmem_limit_bytes=LIMIT),
        cost_estimate=SMALL,
    )(*([] if flag is None else [flag]), *args, *after)


def shape(rows, cols, kind):
    return jax.ShapeDtypeStruct((rows, cols), kind)


def stack_body(*refs):
    out, at = refs[-1], 0
    for ref in refs[:-1]:
        rows = ref.shape[0]
        out[at : at + rows] = ref[...]
        at += rows


def stack(*blocks, after=()):
    rows = sum(b.shape[0] for b in blocks)
    out = shape(rows, blocks[0].shape[1], blocks[0].dtype)
    return local(stack_body, [out], *blocks, after=after)[0]


def sums_body(block, weight, out):
    out[...] = dot_t(block[...], weight[...])


def cut_body(a, b, lo, hi):
    half = lo.shape[0]
    lo[...] = a[:half]
    hi[...] = b[half:]


def split_body(rows_in, flag, *refs):
    n = len(rows_in)
    gus, ghs, (keep, send) = refs[:n], refs[n:-2], refs[-2:]
    first = flag[0] == 0
    at = 0
    for ref, rows in zip(gus, rows_in):
        for i in range(rows // (2 * TOK)):
            a = ref[2 * TOK * i : 2 * TOK * i + TOK]
            b = ref[2 * TOK * i + TOK : 2 * TOK * (i + 1)]
            keep[at : at + TOK, : 2 * FF] = jnp.where(first, a, b)
            send[at : at + TOK, : 2 * FF] = jnp.where(first, b, a)
            at += TOK
    for x, ref in enumerate(ghs):
        for i in range(ref.shape[0] // (2 * TOK)):
            a = ref[2 * TOK * i : 2 * TOK * i + TOK]
            b = ref[2 * TOK * i + TOK : 2 * TOK * (i + 1)]
            at = (i * NX + x) * TOK
            keep[at : at + TOK, 2 * FF :] = jnp.where(first, a, b)
            send[at : at + TOK, 2 * FF :] = jnp.where(first, b, a)


def add_body(a, b, full, low):
    total = a[...] + b[...]
    full[...] = total
    low[...] = total.astype(BF)


def act_body(a, b, out):
    gate = a[:, :FF] + b[:, :FF].astype(F32)
    up = a[:, FF : 2 * FF] + b[:, FF : 2 * FF].astype(F32)
    grad_hidden = a[:, 2 * FF :] + b[:, 2 * FF :].astype(F32)
    sig = 1.0 / (1.0 + jnp.exp(-gate))
    act = gate * sig
    out[:, :FF] = (act * up).astype(BF)
    out[:, FF : 2 * FF] = (grad_hidden * up * sig * (1.0 + gate * (1.0 - sig))).astype(BF)
    out[:, 2 * FF :] = (grad_hidden * act).astype(BF)


def order_body(nz, with_x, flag, mine, theirs, *outs):
    by_z, hid, by_x = outs[:nz], outs[nz : nz + NX], outs[nz + NX :]
    first = flag[0] == 0
    for z in range(nz):
        for x in range(NX):
            at = (z * NX + x) * TOK
            a, b = mine[at : at + TOK], theirs[at : at + TOK]
            for h, val in enumerate((jnp.where(first, a, b), jnp.where(first, b, a))):
                to = (2 * z + h) * TOK
                hid[x][to : to + TOK] = val[:, :FF]
                if with_x:
                    by_x[x][to : to + TOK] = val[:, FF:]
                to = (2 * x + h) * TOK
                by_z[z][to : to + TOK] = val[:, FF:]


def fold_body(own, *refs):
    parts, outs = refs[:-2], refs[-2:]
    for i in range(outs[0].shape[0] // TOK):
        for h, out in enumerate(outs):
            s = slice((2 * i + h) * TOK, (2 * i + h + 1) * TOK)
            total = own[s]
            for part in parts:
                total = total + part[s].astype(F32)
            out[i * TOK : (i + 1) * TOK] = total.astype(out.dtype)


def carry_body(a, b, c, d, lo, hi):
    lo[...] = (a[...] + b[...].astype(F32)).astype(BF)
    hi[...] = (c[...] + d[...].astype(F32)).astype(BF)


def join_body(keep, recv, *outs):
    for i, out in enumerate(outs):
        s = slice(i * TOK, (i + 1) * TOK)
        out[...] = (keep[s] + recv[s].astype(F32)).astype(out.dtype)


def last_body(own, *refs):
    parts, out = refs[:-1], refs[-1]
    total = own[...]
    for part in parts:
        total = total + part[...].astype(F32)
    out[...] = total.astype(BF)


def weight_grad_body(n, los, *refs):
    acts, blocks, outs, mark = refs[:n], refs[n : 2 * n], refs[2 * n : -1], refs[-1]
    mark[...] = jnp.zeros_like(mark)
    left = [jnp.concatenate([a[:, lo : lo + FF] for a in acts]).T for lo in los]

    @pl.loop(0, outs[0].shape[1] // 512)
    def _(j):
        cols = pl.ds(pl.multiple_of(j * 512, 512), 512)
        right = jnp.concatenate([b[:, cols] for b in blocks])
        for lhs, out in zip(left, outs):
            part = jnp.dot(lhs, right, preferred_element_type=F32)
            out[:, cols] = part[: out.shape[0]]


def weight_grad(acts, blocks, los, ff, *after):
    outs = [shape(ff, blocks[0].shape[1], F32)] * len(los) + [shape(8, 128, F32)]
    body = functools.partial(weight_grad_body, len(acts), los)
    return local(body, outs, *acts, *blocks, after=after)


def tie_body(n, *refs):
    refs[-1][...] = jnp.zeros_like(refs[-1])


def tie(values, *after):
    n = len(values)
    *out, mark = pl.pallas_call(
        functools.partial(tie_body, n),
        out_shape=[jax.ShapeDtypeStruct(v.shape, v.dtype) for v in values] + [shape(8, 128, F32)],
        in_specs=[pl.BlockSpec(memory_space=pl.ANY)] * (n + len(after)),
        out_specs=[pl.BlockSpec(memory_space=pl.ANY)] * n + [pl.BlockSpec(memory_space=pltpu.VMEM)],
        input_output_aliases={i: i for i in range(n)},
        compiler_params=pltpu.CompilerParams(vmem_limit_bytes=2**20),
        cost_estimate=SMALL,
    )(*values, *after)
    return out, mark


def pack_body(gate, up, down, weight, down_out):
    ff, width = gate.shape
    pad = jnp.zeros((FF - ff, width), BF)
    weight[:ff] = gate[...]
    weight[ff:FF] = pad
    weight[FF : FF + ff] = up[...]
    weight[FF + ff :] = pad
    down_out[:ff] = down[...]
    down_out[ff:] = pad


def pair_body(own, other, cot_own, cot_other, pair, cot):
    pair[:TOK] = own[...]
    pair[TOK:] = other[...]
    cot[:TOK] = cot_own[...]
    cot[TOK:] = cot_other[...]


def back_body(n, *refs):
    blocks, weight, outs = refs[:n], refs[n], refs[n + 1 :]

    @pl.loop(0, weight.shape[1] // 512)
    def _(j):
        cols = pl.ds(pl.multiple_of(j * 512, 512), 512)
        for block, out in zip(blocks, outs):
            part = jnp.dot(block[...], weight[:, cols], preferred_element_type=F32)
            out[:, cols] = part.astype(out.dtype)


def per_device(stash, grad_out, gate_weight, up_weight, down_weight):
    core = (lax.axis_index("seq") % 2).astype(jnp.int32).reshape(1)
    ff, width = gate_weight.shape
    n = NX * NZ * NH
    own = lax.ppermute(stash, "dp", [(i, (i + 1) % n) for i in range(n)])
    other = lax.ppermute(stash, "dp", [(i, (i + 2 * (i % 2)) % n) for i in range(n)])
    cot_other = hop(grad_out, dh=1)
    weight, down = local(
        pack_body, [shape(2 * FF, width, BF), shape(FF, width, BF)], gate_weight, up_weight, down_weight
    )

    def part(block, after):
        return local(sums_body, [shape(block.shape[0], 2 * FF, F32)], block, weight, after=(after,))[0]

    def cot_part(block, after):
        return local(sums_body, [shape(block.shape[0], FF, F32)], block, down, after=(after,))[0]

    def split(gu, gh):
        tokens = sum(p.shape[0] for p in gu) // 2
        return local(
            functools.partial(split_body, [p.shape[0] for p in gu]),
            [shape(tokens, 3 * FF, F32)] * 2, *gu, *gh, flag=core,
        )

    def chip_sum(keep, recv):
        rows = keep.shape[0]
        return local(add_body, [shape(rows, 3 * FF, F32), shape(rows, 3 * FF, BF)], keep, recv)

    def acts_of(chip, recv, *after):
        return local(act_body, [shape(chip.shape[0], 3 * FF, BF)], chip, recv, after=after)[0]

    def order(acts, theirs, nz, with_x, *after):
        out = local(
            functools.partial(order_body, nz, with_x),
            [shape(NX * 2 * TOK, 2 * FF, BF)] * nz
            + [shape(nz * 2 * TOK, FF, BF)] * NX
            + [shape(nz * 2 * TOK, 2 * FF, BF)] * (NX if with_x else 0),
            acts, theirs, flag=core, after=after,
        )
        out = list(out)
        return out[:nz], out[nz : nz + NX], out[nz + NX :]

    def project(blocks, full):
        rows, n = blocks[0].shape[0], len(blocks)
        outs = [shape(rows, width, F32 if i in full else BF) for i in range(n)]
        return local(functools.partial(back_body, n), outs, *blocks, weight)

    def fold(own, recv, *after):
        rows = own.shape[0] // 2
        outs = [shape(rows, width, F32), shape(rows, width, BF)]
        return local(fold_body, outs, own, *recv, after=after)

    def join(keep, recv, kinds):
        return local(join_body, [shape(TOK, width, k) for k in kinds], keep, recv)

    pair, cot = local(pair_body, [shape(2 * TOK, width, BF)] * 2, own, other, grad_out, cot_other)
    x1, x2, x3 = hop(pair, dx=1), hop(pair, dx=-1), hop(pair, dx=2)
    cu1, cd1, cu2, cd2 = [hop(cot, dz=o) for o in (1, -1, 2, -2)]
    row = stack(pair, x1, x2, x3)
    u1, d1 = hop(row, dz=1), hop(row, dz=-1)
    near = stack(cot, cu1, cd1, cu2, cd2, after=(weight, down))
    near_u, near_d = hop(near, dx=1), hop(near, dx=-1)
    cd3 = hop(cd2, dz=-1)
    (u1, d1, near_u, near_d, cu2, cd3), _ = tie([u1, d1, near_u, near_d, cu2, cd3], near)
    cu3 = hop(cu2, dz=1)
    u2, d2 = hop(u1, dz=1), hop(d1, dz=-1)
    near_f, c4 = hop(near_u, dx=1), hop(cd3, dz=-1)
    (u2, d2, near_f, cu3, c4), _ = tie([u2, d2, near_f, cu3, c4])
    far = stack(cu3, cd3, c4)
    u3, d3 = hop(u2, dz=1), hop(d2, dz=-1)
    far_u, far_d = hop(far, dx=1), hop(far, dx=-1)
    in1, cot1 = [row, u1, d1, u2, d2], [near, near_u, near_d, near_f]
    keep1, send1 = split([dot_t(b, weight) for b in in1], [dot_t(b, down) for b in cot1])
    chip1, low1 = chip_sum(keep1, swap_core(send1))
    (far_u, far_d, their1), mark = tie([far_u, far_d, swap_chip(low1)], u3, d3)
    half = row.shape[0] // 2
    lo, hi = local(cut_body, [shape(half, width, BF)] * 2, u3, d3, after=(mark,))
    f_lo, f_hi, far_f = hop(lo, dz=1), hop(hi, dz=-1), hop(far_d, dx=-1)
    acts1 = acts_of(chip1, their1)

    by_z1, hid1, _ = order(acts1, swap_core(acts1), len(GROUPS[0]), False)
    mine1, one_d, one_u, two_d, two_u = project(by_z1, (0, 1, 2))
    two_d, two_u = hop(two_d, dz=-1), hop(two_u, dz=1)
    gu2 = [part(b, mine1) for b in (u3, d3)]
    gh2 = [cot_part(b, mine1) for b in (far, far_u, far_d)]
    (f_lo, f_hi, far_f), mark = tie([f_lo, f_hi, far_f], *gu2, *gh2)
    in2, cot2 = [u3, d3, f_lo, f_hi], [far, far_u, far_d, far_f]
    gu2 += [part(b, mark) for b in (f_lo, f_hi)]
    keep2, send2 = split(gu2, gh2 + [cot_part(far_f, mark)])
    chip2, low2 = chip_sum(keep2, swap_core(send2))
    one_d, one_u = local(
        carry_body, [shape(8 * TOK, width, BF)] * 2, one_d, two_d, one_u, two_u, after=(low2,)
    )
    acts2 = acts_of(chip2, swap_chip(low2), one_d)
    other2 = swap_core(acts2)
    recv1 = [hop(one_d, dz=-1), hop(one_u, dz=1)]
    by_z2, hid2, by_x2 = order(acts2, other2, len(GROUPS[1]), True, one_d)
    mine2, *out2 = project(by_x2, (0,))
    recv2 = [hop(out2[i - 1], dx=X_OFF[i]) for i in (3, 1, 2)]
    far_row = stack(f_lo, f_hi, after=(mine2,))
    grad_gate, grad_up, mark_a = weight_grad(by_z1 + by_z2, in1 + [u3, d3, far_row], (0, FF), ff)
    grad_down, mark_b = weight_grad(hid1 + hid2, cot1 + cot2, (0,), ff, far_row)
    keep1, send1 = fold(mine1, recv1, mark_a, mark_b)
    keep2, send2 = fold(mine2, recv2, keep1)
    own_sum, *out1 = join(keep1, hop(send1, dh=1), [F32] + [BF] * 3)
    sent = [hop(out1[i - 1], dx=X_OFF[i]) for i in (3, 1, 2)]
    out2 = join(keep2, hop(send2, dh=1), [BF] * 3)
    sent += [hop(b, dz=Z_OFF[z]) for z, b in zip(GROUPS[1], out2)]
    (grad_input,) = local(last_body, [shape(TOK, width, BF)], own_sum, *sent)
    return grad_input, grad_gate, grad_up, grad_down


def solution(mesh):
    spec = P("dp", "seq")
    return jax.shard_map(
        per_device, mesh=mesh, in_specs=(spec,) * 5, out_specs=(spec,) * 4, check_vma=False
    )
```

```python
import functools

import jax
import jax.numpy as jnp
from jax import lax
from jax.experimental import pallas as pl
from jax.experimental.pallas import tpu as pltpu
from jax.sharding import PartitionSpec as P

NX, NZ, NH = 4, 8, 2
BF, F32 = jnp.bfloat16, jnp.float32
Z_OFF = (0, -1, 1, -2, 2, -3, 3, 4)
X_OFF = (0, -1, 1, 2)
GROUPS = ((0, 1, 2, 3, 4), (5, 6, 7))
TOK = 16
FF = 256
LIMIT = 16 * 2**20
SMALL = pl.CostEstimate(flops=1, bytes_accessed=1, transcendentals=0)


def dp_index(x, z, h):
    return ((x % NX) * NZ + z % NZ) * NH + h % NH


def hop(block, dx=0, dz=0, dh=0):
    route = [
        (dp_index(x, z, h), dp_index(x + dx, z + dz, h + dh))
        for x in range(NX)
        for z in range(NZ)
        for h in range(NH)
    ]
    return lax.ppermute(block, "dp", route)


def swap_core(block):
    return lax.ppermute(block, "seq", [(0, 1), (1, 0), (2, 3), (3, 2)])


def swap_chip(block):
    return lax.ppermute(block, "seq", [(0, 2), (2, 0), (1, 3), (3, 1)])


def dot_t(left, right):
    return lax.dot_general(left, right, (((1,), (1,)), ((), ())), preferred_element_type=F32)


def dot_first(left, right):
    return lax.dot_general(left, right, (((0,), (0,)), ((), ())), preferred_element_type=F32)


def local(body, outs, *args, flag=None, after=(), cost=SMALL):
    n, first = len(args), 0 if flag is None else 1

    def run(*refs):
        body(*refs[: n + first], *refs[n + first + len(after) :])

    vmem, free = pl.BlockSpec(memory_space=pltpu.VMEM), pl.BlockSpec(memory_space=pl.ANY)
    return pl.pallas_call(
        run,
        out_shape=list(outs),
        in_specs=[pl.BlockSpec(memory_space=pltpu.SMEM)] * first + [vmem] * n + [free] * len(after),
        out_specs=[vmem] * len(outs),
        compiler_params=pltpu.CompilerParams(vmem_limit_bytes=LIMIT),
        cost_estimate=cost,
    )(*([] if flag is None else [flag]), *args, *after)


def shape(rows, cols, kind):
    return jax.ShapeDtypeStruct((rows, cols), kind)


def stack_body(*refs):
    out, at = refs[-1], 0
    for ref in refs[:-1]:
        rows = ref.shape[0]
        out[at : at + rows] = ref[...]
        at += rows


def stack(*blocks, after=()):
    rows = sum(b.shape[0] for b in blocks)
    out = shape(rows, blocks[0].shape[1], blocks[0].dtype)
    return local(stack_body, [out], *blocks, after=after)[0]


def sums_body(block, weight, out):
    out[...] = dot_t(block[...], weight[...])


def cut_body(a, b, lo, hi):
    half = lo.shape[0]
    lo[...] = a[:half]
    hi[...] = b[half:]


def split_body(rows_in, flag, *refs):
    n = len(rows_in)
    gus, ghs, (keep, send_gu, send_gh) = refs[:n], refs[n:-3], refs[-3:]
    first = flag[0] == 0
    at = 0
    for ref, rows in zip(gus, rows_in):
        for i in range(rows // (2 * TOK)):
            a = ref[2 * TOK * i : 2 * TOK * i + TOK]
            b = ref[2 * TOK * i + TOK : 2 * TOK * (i + 1)]
            keep[at : at + TOK, : 2 * FF] = jnp.where(first, a, b)
            send_gu[at : at + TOK] = jnp.where(first, b, a)
            at += TOK
    for x, ref in enumerate(ghs):
        for i in range(ref.shape[0] // (2 * TOK)):
            a = ref[2 * TOK * i : 2 * TOK * i + TOK]
            b = ref[2 * TOK * i + TOK : 2 * TOK * (i + 1)]
            at = (i * NX + x) * TOK
            keep[at : at + TOK, 2 * FF :] = jnp.where(first, a, b)
            send_gh[at : at + TOK] = jnp.where(first, b, a)


def add_body(a, b_gu, b_gh, full, low):
    for lo, b in ((0, b_gu), (2 * FF, b_gh)):
        hi = lo + b.shape[1]
        total = a[:, lo:hi] + b[...]
        full[:, lo:hi] = total
        low[:, lo:hi] = total.astype(BF)


def act_body(a, b, out):
    gate = a[:, :FF] + b[:, :FF].astype(F32)
    up = a[:, FF : 2 * FF] + b[:, FF : 2 * FF].astype(F32)
    grad_hidden = a[:, 2 * FF :] + b[:, 2 * FF :].astype(F32)
    sig = 1.0 / (1.0 + jnp.exp(-gate))
    act = gate * sig
    out[:, :FF] = (act * up).astype(BF)
    out[:, FF : 2 * FF] = (grad_hidden * up * sig * (1.0 + gate * (1.0 - sig))).astype(BF)
    out[:, 2 * FF :] = (grad_hidden * act).astype(BF)


def order_body(nz, with_x, flag, mine, theirs, *outs):
    by_z, hid, by_x = outs[:nz], outs[nz : nz + NX], outs[nz + NX :]
    first = flag[0] == 0
    for z in range(nz):
        for x in range(NX):
            at = (z * NX + x) * TOK
            a, b = mine[at : at + TOK], theirs[at : at + TOK]
            for h, val in enumerate((jnp.where(first, a, b), jnp.where(first, b, a))):
                to = (2 * z + h) * TOK
                hid[x][to : to + TOK] = val[:, :FF]
                if with_x:
                    by_x[x][to : to + TOK] = val[:, FF:]
                to = (2 * x + h) * TOK
                by_z[z][to : to + TOK] = val[:, FF:]


def fold_body(own, *refs):
    parts, outs = refs[:-2], refs[-2:]
    for i in range(outs[0].shape[0] // TOK):
        for h, out in enumerate(outs):
            s = slice((2 * i + h) * TOK, (2 * i + h + 1) * TOK)
            total = own[s]
            for part in parts:
                total = total + part[s].astype(F32)
            out[i * TOK : (i + 1) * TOK] = total.astype(out.dtype)


def carry_body(a, b, c, d, lo, hi):
    lo[...] = (a[...] + b[...].astype(F32)).astype(BF)
    hi[...] = (c[...] + d[...].astype(F32)).astype(BF)


def join_body(keep, recv, *outs):
    for i, out in enumerate(outs):
        s = slice(i * TOK, (i + 1) * TOK)
        out[...] = (keep[s] + recv[s].astype(F32)).astype(out.dtype)


def last_body(own, *refs):
    parts, out = refs[:-1], refs[-1]
    total = own[...]
    for part in parts:
        total = total + part[...].astype(F32)
    out[...] = total.astype(BF)


def weight_grad_body(n, los, *refs):
    acts, blocks, outs, mark = refs[:n], refs[n : 2 * n], refs[2 * n : -1], refs[-1]
    mark[...] = jnp.zeros_like(mark)
    left = [jnp.concatenate([a[:, lo : lo + FF] for a in acts]).T for lo in los]

    @pl.loop(0, outs[0].shape[1] // 512)
    def _(j):
        cols = pl.ds(pl.multiple_of(j * 512, 512), 512)
        right = jnp.concatenate([b[:, cols] for b in blocks])
        for lhs, out in zip(left, outs):
            part = jnp.dot(lhs, right, preferred_element_type=F32)
            out[:, cols] = part[: out.shape[0]]


def weight_grad(acts, blocks, los, ff, *after, cost=SMALL):
    outs = [shape(ff, blocks[0].shape[1], F32)] * len(los) + [shape(8, 128, F32)]
    body = functools.partial(weight_grad_body, len(acts), los)
    return local(body, outs, *acts, *blocks, after=after, cost=cost)


def tie_body(n, *refs):
    refs[-1][...] = jnp.zeros_like(refs[-1])


def tie(values, *after):
    n = len(values)
    *out, mark = pl.pallas_call(
        functools.partial(tie_body, n),
        out_shape=[jax.ShapeDtypeStruct(v.shape, v.dtype) for v in values] + [shape(8, 128, F32)],
        in_specs=[pl.BlockSpec(memory_space=pl.ANY)] * (n + len(after)),
        out_specs=[pl.BlockSpec(memory_space=pl.ANY)] * n + [pl.BlockSpec(memory_space=pltpu.VMEM)],
        input_output_aliases={i: i for i in range(n)},
        compiler_params=pltpu.CompilerParams(vmem_limit_bytes=2**20),
        cost_estimate=SMALL,
    )(*values, *after)
    return out, mark


def pause(flops, after):
    return pl.pallas_call(
        functools.partial(tie_body, 0),
        out_shape=shape(8, 128, F32),
        in_specs=[pl.BlockSpec(memory_space=pl.ANY)],
        out_specs=pl.BlockSpec(memory_space=pltpu.VMEM),
        compiler_params=pltpu.CompilerParams(vmem_limit_bytes=2**20),
        cost_estimate=pl.CostEstimate(flops=flops, bytes_accessed=1, transcendentals=0),
    )(after)


def pack_body(gate, up, down, weight, down_out):
    ff, width = gate.shape
    pad = jnp.zeros((FF - ff, width), BF)
    weight[:ff] = gate[...]
    weight[ff:FF] = pad
    weight[FF : FF + ff] = up[...]
    weight[FF + ff :] = pad
    down_out[:ff] = down[...]
    down_out[ff:] = pad


def pair_body(own, other, cot_own, cot_other, pair, cot):
    pair[:TOK] = own[...]
    pair[TOK:] = other[...]
    cot[:TOK] = cot_own[...]
    cot[TOK:] = cot_other[...]


def back_body(n, *refs):
    blocks, weight, outs = refs[:n], refs[n], refs[n + 1 :]

    @pl.loop(0, weight.shape[1] // 512)
    def _(j):
        cols = pl.ds(pl.multiple_of(j * 512, 512), 512)
        for block, out in zip(blocks, outs):
            part = jnp.dot(block[...], weight[:, cols], preferred_element_type=F32)
            out[:, cols] = part.astype(out.dtype)


def per_device(stash, grad_out, gate_weight, up_weight, down_weight):
    core = (lax.axis_index("seq") % 2).astype(jnp.int32).reshape(1)
    ff, width = gate_weight.shape
    n = NX * NZ * NH
    own = lax.ppermute(stash, "dp", [(i, (i + 1) % n) for i in range(n)])
    other = lax.ppermute(stash, "dp", [(i, (i + 2 * (i % 2)) % n) for i in range(n)])
    cot_other = hop(grad_out, dh=1)
    weight, down = local(
        pack_body, [shape(2 * FF, width, BF), shape(FF, width, BF)], gate_weight, up_weight, down_weight
    )

    def part(block, after):
        return local(sums_body, [shape(block.shape[0], 2 * FF, F32)], block, weight, after=(after,))[0]

    def cot_part(block, after):
        return local(sums_body, [shape(block.shape[0], FF, F32)], block, down, after=(after,))[0]

    def split(gu, gh, *after):
        tokens = sum(p.shape[0] for p in gu) // 2
        return local(
            functools.partial(split_body, [p.shape[0] for p in gu]),
            [shape(tokens, n * FF, F32) for n in (3, 2, 1)], *gu, *gh, flag=core, after=after,
        )

    def chip_sum(keep, gu, gh):
        rows = keep.shape[0]
        outs = [shape(rows, 3 * FF, F32), shape(rows, 3 * FF, BF)]
        return local(add_body, outs, keep, swap_core(gu), swap_core(gh))

    def acts_of(chip, recv, *after):
        return local(act_body, [shape(chip.shape[0], 3 * FF, BF)], chip, recv, after=after)[0]

    def order(acts, theirs, nz, with_x, *after):
        out = local(
            functools.partial(order_body, nz, with_x),
            [shape(NX * 2 * TOK, 2 * FF, BF)] * nz
            + [shape(nz * 2 * TOK, FF, BF)] * NX
            + [shape(nz * 2 * TOK, 2 * FF, BF)] * (NX if with_x else 0),
            acts, theirs, flag=core, after=after,
        )
        out = list(out)
        return out[:nz], out[nz : nz + NX], out[nz + NX :]

    def project(blocks, full):
        rows, n = blocks[0].shape[0], len(blocks)
        outs = [shape(rows, width, F32 if i in full else BF) for i in range(n)]
        return local(functools.partial(back_body, n), outs, *blocks, weight)

    def fold(own, recv, *after):
        rows = own.shape[0] // 2
        outs = [shape(rows, width, F32), shape(rows, width, BF)]
        return local(fold_body, outs, own, *recv, after=after)

    def join(keep, recv, kinds, *after):
        return local(join_body, [shape(TOK, width, k) for k in kinds], keep, recv, after=after)

    pair, cot = local(pair_body, [shape(2 * TOK, width, BF)] * 2, own, other, grad_out, cot_other)
    x1, x2, x3 = hop(pair, dx=1), hop(pair, dx=-1), hop(pair, dx=2)
    cu1, cd1, cu2, cd2 = [hop(cot, dz=o) for o in (1, -1, 2, -2)]
    row = stack(pair, x1, x2, x3)
    u1, d1 = hop(row, dz=1), hop(row, dz=-1)
    near = stack(cot, cu1, cd1, cu2, cd2, after=(weight, down))
    near_u, near_d = hop(near, dx=1), hop(near, dx=-1)
    cd3 = hop(cd2, dz=-1)
    (u1, d1, near_u, near_d, cu2, cd3), _ = tie([u1, d1, near_u, near_d, cu2, cd3], near)
    cu3 = hop(cu2, dz=1)
    u2, d2 = hop(u1, dz=1), hop(d1, dz=-1)
    near_f, c4 = hop(near_u, dx=1), hop(cd3, dz=-1)
    (u2, d2, near_f, cu3, c4), _ = tie([u2, d2, near_f, cu3, c4])
    far = stack(cu3, cd3, c4)
    u3, d3 = hop(u2, dz=1), hop(d2, dz=-1)
    far_u, far_d = hop(far, dx=1), hop(far, dx=-1)
    in1, cot1 = [row, u1, d1, u2, d2], [near, near_u, near_d, near_f]
    gu1, gh1 = [dot_t(b, weight) for b in in1], [dot_t(b, down) for b in cot1]
    (far_u, far_d), mark = tie([far_u, far_d], u3, d3, gu1[-1], gh1[-1])
    half = row.shape[0] // 2
    lo, hi = local(cut_body, [shape(half, width, BF)] * 2, u3, d3, after=(mark,))
    f_lo, f_hi, far_f = hop(lo, dz=1), hop(hi, dz=-1), hop(far_d, dx=-1)
    chip1, low1 = chip_sum(*split(gu1, gh1, lo))
    their1 = swap_chip(low1)
    gu2 = [part(b, low1) for b in (u3, d3)]
    gh2 = [cot_part(b, low1) for b in (far, far_u, far_d)]
    (f_lo, f_hi, far_f), mark = tie([f_lo, f_hi, far_f], *gu2, *gh2)
    in2, cot2 = [u3, d3, f_lo, f_hi], [far, far_u, far_d, far_f]
    gu2 += [part(b, mark) for b in (f_lo, f_hi)]
    chip2, low2 = chip_sum(*split(gu2, gh2 + [cot_part(far_f, mark)]))
    their2 = swap_chip(low2)
    acts1 = acts_of(chip1, their1, low2)

    by_z1, hid1, _ = order(acts1, swap_core(acts1), len(GROUPS[0]), False)
    mine1, one_d, one_u, two_d, two_u = project(by_z1, (0, 1, 2))
    two_d, two_u = hop(two_d, dz=-1), hop(two_u, dz=1)
    acts2 = acts_of(chip2, their2, mine1)
    by_z2, hid2, by_x2 = order(acts2, swap_core(acts2), len(GROUPS[1]), True)
    mine2, *out2 = project(by_x2, (0,))
    recv2 = [hop(out2[i - 1], dx=X_OFF[i]) for i in (3, 1, 2)]
    one_d, one_u = local(
        carry_body, [shape(8 * TOK, width, BF)] * 2, one_d, two_d, one_u, two_u, after=(mine2,)
    )
    recv1 = [hop(one_d, dz=-1), hop(one_u, dz=1)]
    far_row = stack(f_lo, f_hi, after=(one_d,))
    grad_gate, grad_up, mark_a = weight_grad(by_z1 + by_z2, in1 + [u3, d3, far_row], (0, FF), ff)
    keep2, send2 = fold(mine2, recv2, mark_a)
    cost = pl.CostEstimate(flops=4_600_000_000, bytes_accessed=1, transcendentals=0)
    grad_down, mark_b = weight_grad(hid1 + hid2, cot1 + cot2, (0,), ff, keep2, cost=cost)
    keep1, send1 = fold(mine1, recv1, mark_b)
    out2 = join(keep2, hop(send2, dh=1), [BF] * 3)
    sent = [hop(b, dz=Z_OFF[z]) for z, b in zip(GROUPS[1], out2)]
    own_sum, *out1 = join(keep1, hop(send1, dh=1), [F32] + [BF] * 3, pause(2_300_000_000, out2[0]))
    sent += [hop(out1[i - 1], dx=X_OFF[i]) for i in (3, 1, 2)]
    (grad_input,) = local(last_body, [shape(TOK, width, BF)], own_sum, *sent)
    return grad_input, grad_gate, grad_up, grad_down


def solution(mesh):
    spec = P("dp", "seq")
    return jax.shard_map(
        per_device, mesh=mesh, in_specs=(spec,) * 5, out_specs=(spec,) * 4, check_vma=False
    )
```

```python
import functools

import jax
import jax.numpy as jnp
from jax import lax
from jax.experimental import pallas as pl
from jax.experimental.pallas import tpu as pltpu
from jax.sharding import PartitionSpec as P

NX, NZ, NH = 4, 8, 2
BF, F32 = jnp.bfloat16, jnp.float32
Z_OFF = (0, -1, 1, -2, 2, -3, 3, 4)
X_OFF = (0, -1, 1, 2)
GROUPS = ((0, 1, 2, 3, 4), (5, 6, 7))
TOK = 16
FF = 256
LIMIT = 16 * 2**20
SMALL = pl.CostEstimate(flops=1, bytes_accessed=1, transcendentals=0)


def dp_index(x, z, h):
    return ((x % NX) * NZ + z % NZ) * NH + h % NH


def hop(block, dx=0, dz=0, dh=0):
    route = [
        (dp_index(x, z, h), dp_index(x + dx, z + dz, h + dh))
        for x in range(NX)
        for z in range(NZ)
        for h in range(NH)
    ]
    return lax.ppermute(block, "dp", route)


def swap_core(block):
    return lax.ppermute(block, "seq", [(0, 1), (1, 0), (2, 3), (3, 2)])


def swap_chip(block):
    return lax.ppermute(block, "seq", [(0, 2), (2, 0), (1, 3), (3, 1)])


def dot_t(left, right):
    return lax.dot_general(left, right, (((1,), (1,)), ((), ())), preferred_element_type=F32)


def dot_first(left, right):
    return lax.dot_general(left, right, (((0,), (0,)), ((), ())), preferred_element_type=F32)


def local(body, outs, *args, flag=None, after=(), cost=SMALL):
    n, first = len(args), 0 if flag is None else 1

    def run(*refs):
        body(*refs[: n + first], *refs[n + first + len(after) :])

    vmem, free = pl.BlockSpec(memory_space=pltpu.VMEM), pl.BlockSpec(memory_space=pl.ANY)
    return pl.pallas_call(
        run,
        out_shape=list(outs),
        in_specs=[pl.BlockSpec(memory_space=pltpu.SMEM)] * first + [vmem] * n + [free] * len(after),
        out_specs=[vmem] * len(outs),
        compiler_params=pltpu.CompilerParams(vmem_limit_bytes=LIMIT),
        cost_estimate=cost,
    )(*([] if flag is None else [flag]), *args, *after)


def shape(rows, cols, kind):
    return jax.ShapeDtypeStruct((rows, cols), kind)


def stack_body(*refs):
    out, at = refs[-1], 0
    for ref in refs[:-1]:
        rows = ref.shape[0]
        out[at : at + rows] = ref[...]
        at += rows


def stack(*blocks, after=()):
    rows = sum(b.shape[0] for b in blocks)
    out = shape(rows, blocks[0].shape[1], blocks[0].dtype)
    return local(stack_body, [out], *blocks, after=after)[0]


def sums_body(block, weight, out):
    out[...] = dot_t(block[...], weight[...])


def cut_body(a, b, lo, hi):
    half = lo.shape[0]
    lo[...] = a[:half]
    hi[...] = b[half:]


def split_body(rows_in, flag, *refs):
    n = len(rows_in)
    gus, ghs, (keep, send_g, send_u, send_h) = refs[:n], refs[n:-4], refs[-4:]
    first = flag[0] == 0
    at = 0
    for ref, rows in zip(gus, rows_in):
        for i in range(rows // (2 * TOK)):
            a = ref[2 * TOK * i : 2 * TOK * i + TOK]
            b = ref[2 * TOK * i + TOK : 2 * TOK * (i + 1)]
            keep[at : at + TOK, : 2 * FF] = jnp.where(first, a, b)
            send = jnp.where(first, b, a)
            send_g[at : at + TOK], send_u[at : at + TOK] = send[:, :FF], send[:, FF:]
            at += TOK
    for x, ref in enumerate(ghs):
        for i in range(ref.shape[0] // (2 * TOK)):
            a = ref[2 * TOK * i : 2 * TOK * i + TOK]
            b = ref[2 * TOK * i + TOK : 2 * TOK * (i + 1)]
            at = (i * NX + x) * TOK
            keep[at : at + TOK, 2 * FF :] = jnp.where(first, a, b)
            send_h[at : at + TOK] = jnp.where(first, b, a)


def add_body(a, g, u, h, full, low):
    for lo, b in ((0, g), (FF, u), (2 * FF, h)):
        hi = lo + FF
        total = a[:, lo:hi] + b[...]
        full[:, lo:hi] = total
        low[:, lo:hi] = total.astype(BF)


def act_body(a, b, out):
    gate = a[:, :FF] + b[:, :FF].astype(F32)
    up = a[:, FF : 2 * FF] + b[:, FF : 2 * FF].astype(F32)
    grad_hidden = a[:, 2 * FF :] + b[:, 2 * FF :].astype(F32)
    sig = 1.0 / (1.0 + jnp.exp(-gate))
    act = gate * sig
    out[:, :FF] = (act * up).astype(BF)
    out[:, FF : 2 * FF] = (grad_hidden * up * sig * (1.0 + gate * (1.0 - sig))).astype(BF)
    out[:, 2 * FF :] = (grad_hidden * act).astype(BF)


def order_body(nz, with_x, flag, mine, theirs, *outs):
    by_z, hid, by_x = outs[:nz], outs[nz : nz + NX], outs[nz + NX :]
    first = flag[0] == 0
    for z in range(nz):
        for x in range(NX):
            at = (z * NX + x) * TOK
            a, b = mine[at : at + TOK], theirs[at : at + TOK]
            for h, val in enumerate((jnp.where(first, a, b), jnp.where(first, b, a))):
                to = (2 * z + h) * TOK
                hid[x][to : to + TOK] = val[:, :FF]
                if with_x:
                    by_x[x][to : to + TOK] = val[:, FF:]
                to = (2 * x + h) * TOK
                by_z[z][to : to + TOK] = val[:, FF:]


def fold_body(own, *refs):
    parts, outs = refs[:-2], refs[-2:]
    for i in range(outs[0].shape[0] // TOK):
        for h, out in enumerate(outs):
            s = slice((2 * i + h) * TOK, (2 * i + h + 1) * TOK)
            total = own[s]
            for part in parts:
                total = total + part[s].astype(F32)
            out[i * TOK : (i + 1) * TOK] = total.astype(out.dtype)


def carry_body(a, b, c, d, lo, hi):
    lo[...] = (a[...] + b[...].astype(F32)).astype(BF)
    hi[...] = (c[...] + d[...].astype(F32)).astype(BF)


def join_body(keep, recv, *outs):
    for i, out in enumerate(outs):
        s = slice(i * TOK, (i + 1) * TOK)
        out[...] = (keep[s] + recv[s].astype(F32)).astype(out.dtype)


def last_body(own, *refs):
    parts, out = refs[:-1], refs[-1]
    total = own[...]
    for part in parts:
        total = total + part[...].astype(F32)
    out[...] = total.astype(BF)


def weight_grad_body(n, los, *refs):
    acts, blocks, outs, mark = refs[:n], refs[n : 2 * n], refs[2 * n : -1], refs[-1]
    mark[...] = jnp.zeros_like(mark)
    left = [jnp.concatenate([a[:, lo : lo + FF] for a in acts]).T for lo in los]

    @pl.loop(0, outs[0].shape[1] // 512)
    def _(j):
        cols = pl.ds(pl.multiple_of(j * 512, 512), 512)
        right = jnp.concatenate([b[:, cols] for b in blocks])
        for lhs, out in zip(left, outs):
            part = jnp.dot(lhs, right, preferred_element_type=F32)
            out[:, cols] = part[: out.shape[0]]


def weight_grad(acts, blocks, los, ff, *after, cost=SMALL):
    outs = [shape(ff, blocks[0].shape[1], F32)] * len(los) + [shape(8, 128, F32)]
    body = functools.partial(weight_grad_body, len(acts), los)
    return local(body, outs, *acts, *blocks, after=after, cost=cost)


def tie_body(n, *refs):
    refs[-1][...] = jnp.zeros_like(refs[-1])


def tie(values, *after):
    n = len(values)
    *out, mark = pl.pallas_call(
        functools.partial(tie_body, n),
        out_shape=[jax.ShapeDtypeStruct(v.shape, v.dtype) for v in values] + [shape(8, 128, F32)],
        in_specs=[pl.BlockSpec(memory_space=pl.ANY)] * (n + len(after)),
        out_specs=[pl.BlockSpec(memory_space=pl.ANY)] * n + [pl.BlockSpec(memory_space=pltpu.VMEM)],
        input_output_aliases={i: i for i in range(n)},
        compiler_params=pltpu.CompilerParams(vmem_limit_bytes=2**20),
        cost_estimate=SMALL,
    )(*values, *after)
    return out, mark


def pause(flops, after):
    return pl.pallas_call(
        functools.partial(tie_body, 0),
        out_shape=shape(8, 128, F32),
        in_specs=[pl.BlockSpec(memory_space=pl.ANY)],
        out_specs=pl.BlockSpec(memory_space=pltpu.VMEM),
        compiler_params=pltpu.CompilerParams(vmem_limit_bytes=2**20),
        cost_estimate=pl.CostEstimate(flops=flops, bytes_accessed=1, transcendentals=0),
    )(after)


def pack_body(gate, up, down, weight, down_out):
    ff, width = gate.shape
    pad = jnp.zeros((FF - ff, width), BF)
    weight[:ff] = gate[...]
    weight[ff:FF] = pad
    weight[FF : FF + ff] = up[...]
    weight[FF + ff :] = pad
    down_out[:ff] = down[...]
    down_out[ff:] = pad


def pair_body(own, other, cot_own, cot_other, pair, cot):
    pair[:TOK] = own[...]
    pair[TOK:] = other[...]
    cot[:TOK] = cot_own[...]
    cot[TOK:] = cot_other[...]


def back_body(n, *refs):
    blocks, weight, outs = refs[:n], refs[n], refs[n + 1 :]

    @pl.loop(0, weight.shape[1] // 512)
    def _(j):
        cols = pl.ds(pl.multiple_of(j * 512, 512), 512)
        for block, out in zip(blocks, outs):
            part = jnp.dot(block[...], weight[:, cols], preferred_element_type=F32)
            out[:, cols] = part.astype(out.dtype)


def per_device(stash, grad_out, gate_weight, up_weight, down_weight):
    core = (lax.axis_index("seq") % 2).astype(jnp.int32).reshape(1)
    ff, width = gate_weight.shape
    n = NX * NZ * NH
    own = lax.ppermute(stash, "dp", [(i, (i + 1) % n) for i in range(n)])
    other = lax.ppermute(stash, "dp", [(i, (i + 2 * (i % 2)) % n) for i in range(n)])
    cot_other = hop(grad_out, dh=1)
    weight, down = local(
        pack_body, [shape(2 * FF, width, BF), shape(FF, width, BF)], gate_weight, up_weight, down_weight
    )

    def part(block, after):
        return local(sums_body, [shape(block.shape[0], 2 * FF, F32)], block, weight, after=(after,))[0]

    def cot_part(block, after):
        return local(sums_body, [shape(block.shape[0], FF, F32)], block, down, after=(after,))[0]

    def split(gu, gh, *after):
        tokens = sum(p.shape[0] for p in gu) // 2
        return local(
            functools.partial(split_body, [p.shape[0] for p in gu]),
            [shape(tokens, n * FF, F32) for n in (3, 1, 1, 1)], *gu, *gh, flag=core, after=after,
        )

    def chip_sum(keep, *sends):
        rows = keep.shape[0]
        outs = [shape(rows, 3 * FF, F32), shape(rows, 3 * FF, BF)]
        return local(add_body, outs, keep, *[swap_core(b) for b in sends])

    def acts_of(chip, recv, *after):
        return local(act_body, [shape(chip.shape[0], 3 * FF, BF)], chip, recv, after=after)[0]

    def order(acts, theirs, nz, with_x, *after):
        out = local(
            functools.partial(order_body, nz, with_x),
            [shape(NX * 2 * TOK, 2 * FF, BF)] * nz
            + [shape(nz * 2 * TOK, FF, BF)] * NX
            + [shape(nz * 2 * TOK, 2 * FF, BF)] * (NX if with_x else 0),
            acts, theirs, flag=core, after=after,
        )
        out = list(out)
        return out[:nz], out[nz : nz + NX], out[nz + NX :]

    def project(blocks, full):
        rows, n = blocks[0].shape[0], len(blocks)
        outs = [shape(rows, width, F32 if i in full else BF) for i in range(n)]
        return local(functools.partial(back_body, n), outs, *blocks, weight)

    def fold(own, recv, *after):
        rows = own.shape[0] // 2
        outs = [shape(rows, width, F32), shape(rows, width, BF)]
        return local(fold_body, outs, own, *recv, after=after)

    def join(keep, recv, kinds, *after):
        return local(join_body, [shape(TOK, width, k) for k in kinds], keep, recv, after=after)

    pair, cot = local(
        pair_body, [shape(2 * TOK, width, BF)] * 2, own, other, grad_out, cot_other, after=(weight, down)
    )
    x1, x2, x3 = hop(pair, dx=1), hop(pair, dx=-1), hop(pair, dx=2)
    cu1, cd1, cu2, cd2 = [hop(cot, dz=o) for o in (1, -1, 2, -2)]
    row = stack(pair, x1, x2, x3)
    u1, d1 = hop(row, dz=1), hop(row, dz=-1)
    near = stack(cot, cu1, cd1, cu2, cd2)
    near_u, near_d = hop(near, dx=1), hop(near, dx=-1)
    cd3 = hop(cd2, dz=-1)
    (u1, d1, near_u, near_d, cu2, cd3), _ = tie([u1, d1, near_u, near_d, cu2, cd3], near)
    cu3 = hop(cu2, dz=1)
    u2, d2 = hop(u1, dz=1), hop(d1, dz=-1)
    near_f, c4 = hop(near_u, dx=1), hop(cd3, dz=-1)
    (u2, d2, near_f, cu3, c4), _ = tie([u2, d2, near_f, cu3, c4])
    far = stack(cu3, cd3, c4)
    u3, d3 = hop(u2, dz=1), hop(d2, dz=-1)
    far_u, far_d = hop(far, dx=1), hop(far, dx=-1)
    in1, cot1 = [row, u1, d1, u2, d2], [near, near_u, near_d, near_f]
    gu1, gh1 = [dot_t(b, weight) for b in in1], [dot_t(b, down) for b in cot1]
    (far_u, far_d), mark = tie([far_u, far_d], gu1[-1], gh1[-1])
    chip1, low1 = chip_sum(*split(gu1, gh1, mark))
    their1 = swap_chip(low1)
    half = row.shape[0] // 2
    lo, hi = local(cut_body, [shape(half, width, BF)] * 2, u3, d3, after=(low1,))
    f_lo, f_hi, far_f = hop(lo, dz=1), hop(hi, dz=-1), hop(far_d, dx=-1)
    gu2 = [part(b, lo) for b in (u3, d3)]
    gh2 = [cot_part(b, lo) for b in (far, far_u, far_d)]
    (f_lo, f_hi, far_f), mark = tie([f_lo, f_hi, far_f], *gu2, *gh2)
    in2, cot2 = [u3, d3, f_lo, f_hi], [far, far_u, far_d, far_f]
    gu2 += [part(b, mark) for b in (f_lo, f_hi)]
    chip2, low2 = chip_sum(*split(gu2, gh2 + [cot_part(far_f, mark)]))
    their2 = swap_chip(low2)
    acts1 = acts_of(chip1, their1, low2)

    by_z1, hid1, _ = order(acts1, swap_core(acts1), len(GROUPS[0]), False)
    mine1, one_d, one_u, two_d, two_u = project(by_z1, (0, 1, 2))
    two_d, two_u = hop(two_d, dz=-1), hop(two_u, dz=1)
    acts2 = acts_of(chip2, their2, mine1)
    by_z2, hid2, by_x2 = order(acts2, swap_core(acts2), len(GROUPS[1]), True)
    mine2, *out2 = project(by_x2, (0,))
    recv2 = [hop(out2[i - 1], dx=X_OFF[i]) for i in (3, 1, 2)]
    one_d, one_u = local(
        carry_body, [shape(8 * TOK, width, BF)] * 2, one_d, two_d, one_u, two_u, after=(mine2,)
    )
    recv1 = [hop(one_d, dz=-1), hop(one_u, dz=1)]
    far_row = stack(f_lo, f_hi, after=(one_d,))
    grad_gate, grad_up, mark_a = weight_grad(by_z1 + by_z2, in1 + [u3, d3, far_row], (0, FF), ff)
    grad_down, mark_b = weight_grad(hid1 + hid2, cot1 + cot2, (0,), ff, mark_a)
    keep2, send2 = fold(mine2, recv2, mark_b)
    keep1, send1 = fold(mine1, recv1, pause(1_850_000_000, keep2))
    out2 = join(keep2, hop(send2, dh=1), [BF] * 3)
    sent = [hop(b, dz=Z_OFF[z]) for z, b in zip(GROUPS[1], out2)]
    own_sum, *out1 = join(keep1, hop(send1, dh=1), [F32] + [BF] * 3, pause(2_300_000_000, out2[0]))
    sent += [hop(out1[i - 1], dx=X_OFF[i]) for i in (3, 1, 2)]
    (grad_input,) = local(last_body, [shape(TOK, width, BF)], own_sum, *sent)
    return grad_input, grad_gate, grad_up, grad_down


def solution(mesh):
    spec = P("dp", "seq")
    return jax.shard_map(
        per_device, mesh=mesh, in_specs=(spec,) * 5, out_specs=(spec,) * 4, check_vma=False
    )
```

```python
import functools

import jax
import jax.numpy as jnp
from jax import lax
from jax.experimental import pallas as pl
from jax.experimental.pallas import tpu as pltpu
from jax.sharding import PartitionSpec as P

NX, NZ, NH = 4, 8, 2
BF, F32 = jnp.bfloat16, jnp.float32
Z_OFF = (0, -1, 1, -2, 2, -3, 3, 4)
X_OFF = (0, -1, 1, 2)
GROUPS = ((0, 1, 2, 3, 4), (5, 6, 7))
TOK = 16
FF = 256
LIMIT = 16 * 2**20
SMALL = pl.CostEstimate(flops=1, bytes_accessed=1, transcendentals=0)


def dp_index(x, z, h):
    return ((x % NX) * NZ + z % NZ) * NH + h % NH


def hop(block, dx=0, dz=0, dh=0):
    route = [
        (dp_index(x, z, h), dp_index(x + dx, z + dz, h + dh))
        for x in range(NX)
        for z in range(NZ)
        for h in range(NH)
    ]
    return lax.ppermute(block, "dp", route)


def swap_core(block):
    return lax.ppermute(block, "seq", [(0, 1), (1, 0), (2, 3), (3, 2)])


def swap_chip(block):
    return lax.ppermute(block, "seq", [(0, 2), (2, 0), (1, 3), (3, 1)])


def dot_t(left, right):
    return lax.dot_general(left, right, (((1,), (1,)), ((), ())), preferred_element_type=F32)


def dot_first(left, right):
    return lax.dot_general(left, right, (((0,), (0,)), ((), ())), preferred_element_type=F32)


def local(body, outs, *args, flag=None, after=(), cost=SMALL):
    n, first = len(args), 0 if flag is None else 1

    def run(*refs):
        body(*refs[: n + first], *refs[n + first + len(after) :])

    vmem, free = pl.BlockSpec(memory_space=pltpu.VMEM), pl.BlockSpec(memory_space=pl.ANY)
    return pl.pallas_call(
        run,
        out_shape=list(outs),
        in_specs=[pl.BlockSpec(memory_space=pltpu.SMEM)] * first + [vmem] * n + [free] * len(after),
        out_specs=[vmem] * len(outs),
        compiler_params=pltpu.CompilerParams(vmem_limit_bytes=LIMIT),
        cost_estimate=cost,
    )(*([] if flag is None else [flag]), *args, *after)


def shape(rows, cols, kind):
    return jax.ShapeDtypeStruct((rows, cols), kind)


def stack_body(*refs):
    out, at = refs[-1], 0
    for ref in refs[:-1]:
        rows = ref.shape[0]
        out[at : at + rows] = ref[...]
        at += rows


def stack(*blocks, after=()):
    rows = sum(b.shape[0] for b in blocks)
    out = shape(rows, blocks[0].shape[1], blocks[0].dtype)
    return local(stack_body, [out], *blocks, after=after)[0]


def sums_body(block, weight, out):
    out[...] = dot_t(block[...], weight[...])


def cut_body(a, b, lo, hi):
    half = lo.shape[0]
    lo[...] = a[:half]
    hi[...] = b[half:]


def split_body(rows_in, flag, *refs):
    n = len(rows_in)
    gus, ghs, (keep, send_g, send_u, send_h) = refs[:n], refs[n:-4], refs[-4:]
    first = flag[0] == 0
    at = 0
    for ref, rows in zip(gus, rows_in):
        for i in range(rows // (2 * TOK)):
            a = ref[2 * TOK * i : 2 * TOK * i + TOK]
            b = ref[2 * TOK * i + TOK : 2 * TOK * (i + 1)]
            keep[at : at + TOK, : 2 * FF] = jnp.where(first, a, b)
            send = jnp.where(first, b, a)
            send_g[at : at + TOK], send_u[at : at + TOK] = send[:, :FF], send[:, FF:]
            at += TOK
    for x, ref in enumerate(ghs):
        for i in range(ref.shape[0] // (2 * TOK)):
            a = ref[2 * TOK * i : 2 * TOK * i + TOK]
            b = ref[2 * TOK * i + TOK : 2 * TOK * (i + 1)]
            at = (i * NX + x) * TOK
            keep[at : at + TOK, 2 * FF :] = jnp.where(first, a, b)
            send_h[at : at + TOK] = jnp.where(first, b, a)


def add_body(a, g, u, h, full, low):
    for lo, b in ((0, g), (FF, u), (2 * FF, h)):
        hi = lo + FF
        total = a[:, lo:hi] + b[...]
        full[:, lo:hi] = total
        low[:, lo:hi] = total.astype(BF)


def act_body(a, b, out):
    gate = a[:, :FF] + b[:, :FF].astype(F32)
    up = a[:, FF : 2 * FF] + b[:, FF : 2 * FF].astype(F32)
    grad_hidden = a[:, 2 * FF :] + b[:, 2 * FF :].astype(F32)
    sig = 1.0 / (1.0 + jnp.exp(-gate))
    act = gate * sig
    out[:, :FF] = (act * up).astype(BF)
    out[:, FF : 2 * FF] = (grad_hidden * up * sig * (1.0 + gate * (1.0 - sig))).astype(BF)
    out[:, 2 * FF :] = (grad_hidden * act).astype(BF)


def order_body(nz, with_x, flag, mine, theirs, *outs):
    by_z, hid, by_x = outs[:nz], outs[nz : nz + NX], outs[nz + NX :]
    first = flag[0] == 0
    for z in range(nz):
        for x in range(NX):
            at = (z * NX + x) * TOK
            a, b = mine[at : at + TOK], theirs[at : at + TOK]
            for h, val in enumerate((jnp.where(first, a, b), jnp.where(first, b, a))):
                to = (2 * z + h) * TOK
                hid[x][to : to + TOK] = val[:, :FF]
                if with_x:
                    by_x[x][to : to + TOK] = val[:, FF:]
                to = (2 * x + h) * TOK
                by_z[z][to : to + TOK] = val[:, FF:]


def fold_body(own, *refs):
    parts, outs = refs[:-2], refs[-2:]
    for i in range(outs[0].shape[0] // TOK):
        for h, out in enumerate(outs):
            s = slice((2 * i + h) * TOK, (2 * i + h + 1) * TOK)
            total = own[s]
            for part in parts:
                total = total + part[s].astype(F32)
            out[i * TOK : (i + 1) * TOK] = total.astype(out.dtype)


def cross_body(*refs):
    blocks, weight, lefts, (keep, send) = refs[:NX], refs[NX], refs[NX + 1 : -2], refs[-2:]
    half, rows = weight.shape[1] // 2, keep.shape[0] // NX

    @pl.loop(0, half // 512)
    def _(j):
        cols = pl.ds(pl.multiple_of(j * 512, 512), 512)
        right = pl.ds(pl.multiple_of(half + j * 512, 512), 512)
        for x, (block, out) in enumerate(zip(blocks, lefts)):
            part = jnp.dot(block[...], weight[:, cols], preferred_element_type=F32)
            out[:, cols] = part.astype(out.dtype)
            part = jnp.dot(block[...], weight[:, right], preferred_element_type=F32)
            for i in range(rows // TOK):
                to = x * rows + i * TOK
                keep[to : to + TOK, cols] = part[2 * i * TOK : (2 * i + 1) * TOK]
                send[to : to + TOK, cols] = part[(2 * i + 1) * TOK : (2 * i + 2) * TOK].astype(BF)


def merge_body(keep, recv, own, a, b, c, *outs):
    half = keep.shape[1]
    for i, out in enumerate(outs):
        s = slice(i * TOK, (i + 1) * TOK)
        out[:, :half] = (keep[s] + recv[s].astype(F32)).astype(BF)
        total = own[s] + a[s].astype(F32) + b[s].astype(F32) + c[s].astype(F32)
        out[:, half:] = total.astype(BF)


def carry_body(a, b, c, d, lo, hi):
    lo[...] = (a[...] + b[...].astype(F32)).astype(BF)
    hi[...] = (c[...] + d[...].astype(F32)).astype(BF)


def join_body(keep, recv, *outs):
    for i, out in enumerate(outs):
        rows = out.shape[0]
        s = slice(i * rows, (i + 1) * rows)
        out[...] = (keep[s] + recv[s].astype(F32)).astype(out.dtype)


def last_body(own, *refs):
    parts, out = refs[:-1], refs[-1]
    total = own[...]
    for part in parts:
        total = total + part[...].astype(F32)
    out[...] = total.astype(BF)


def weight_grad_body(n, los, refs_after, *refs):
    acts, blocks, rest = refs[:n], refs[n : 2 * n], refs[2 * n + refs_after :]
    outs, mark, held, sems = rest[: len(los)], rest[len(los)], rest[len(los) + 1 : -1], rest[-1]
    mark[...] = jnp.zeros_like(mark)
    left = [jnp.concatenate([a[:, lo : lo + FF] for a in acts]) for lo in los]
    copies, tile = [], 1024
    for j in range(held[0].shape[1] // tile):
        cols = slice(j * tile, (j + 1) * tile)
        right = jnp.concatenate([b[:, cols] for b in blocks])
        for i, (lhs, out, buf) in enumerate(zip(left, outs, held)):
            buf[:, cols] = dot_first(lhs, right)[: buf.shape[0]]
            copies.append(pltpu.make_async_copy(buf.at[:, cols], out.at[:, cols], sems.at[i, j]))
            copies[-1].start()
    for copy in copies:
        copy.wait()


def weight_grad(acts, blocks, los, ff, *after):
    vmem, free = pl.BlockSpec(memory_space=pltpu.VMEM), pl.BlockSpec(memory_space=pl.ANY)
    n, width = len(acts), blocks[0].shape[1]
    return pl.pallas_call(
        functools.partial(weight_grad_body, n, los, len(after)),
        out_shape=[shape(ff, width, F32)] * len(los) + [shape(8, 128, F32)],
        in_specs=[vmem] * (2 * n) + [free] * len(after),
        out_specs=[free] * len(los) + [vmem],
        scratch_shapes=[pltpu.VMEM((ff, width), F32)] * len(los)
        + [pltpu.SemaphoreType.DMA((len(los), width // 1024))],
        compiler_params=pltpu.CompilerParams(vmem_limit_bytes=LIMIT),
        cost_estimate=SMALL,
    )(*acts, *blocks, *after)


def tie_body(n, *refs):
    refs[-1][...] = jnp.zeros_like(refs[-1])


def tie(values, *after):
    n = len(values)
    *out, mark = pl.pallas_call(
        functools.partial(tie_body, n),
        out_shape=[jax.ShapeDtypeStruct(v.shape, v.dtype) for v in values] + [shape(8, 128, F32)],
        in_specs=[pl.BlockSpec(memory_space=pl.ANY)] * (n + len(after)),
        out_specs=[pl.BlockSpec(memory_space=pl.ANY)] * n + [pl.BlockSpec(memory_space=pltpu.VMEM)],
        input_output_aliases={i: i for i in range(n)},
        compiler_params=pltpu.CompilerParams(vmem_limit_bytes=2**20),
        cost_estimate=SMALL,
    )(*values, *after)
    return out, mark


def pause(flops, after):
    return pl.pallas_call(
        functools.partial(tie_body, 0),
        out_shape=shape(8, 128, F32),
        in_specs=[pl.BlockSpec(memory_space=pl.ANY)],
        out_specs=pl.BlockSpec(memory_space=pltpu.VMEM),
        compiler_params=pltpu.CompilerParams(vmem_limit_bytes=2**20),
        cost_estimate=pl.CostEstimate(flops=flops, bytes_accessed=1, transcendentals=0),
    )(after)


def pack_body(gate, up, down, weight, down_out):
    ff, width = gate.shape
    pad = jnp.zeros((FF - ff, width), BF)
    weight[:ff] = gate[...]
    weight[ff:FF] = pad
    weight[FF : FF + ff] = up[...]
    weight[FF + ff :] = pad
    down_out[:ff] = down[...]
    down_out[ff:] = pad


def pair_body(own, other, cot_own, cot_other, pair, cot):
    pair[:TOK] = own[...]
    pair[TOK:] = other[...]
    cot[:TOK] = cot_own[...]
    cot[TOK:] = cot_other[...]


def back_body(n, *refs):
    blocks, weight, outs = refs[:n], refs[n], refs[n + 1 :]

    @pl.loop(0, weight.shape[1] // 512)
    def _(j):
        cols = pl.ds(pl.multiple_of(j * 512, 512), 512)
        for block, out in zip(blocks, outs):
            part = jnp.dot(block[...], weight[:, cols], preferred_element_type=F32)
            out[:, cols] = part.astype(out.dtype)


def per_device(stash, grad_out, gate_weight, up_weight, down_weight):
    core = (lax.axis_index("seq") % 2).astype(jnp.int32).reshape(1)
    ff, width = gate_weight.shape
    n = NX * NZ * NH
    own = lax.ppermute(stash, "dp", [(i, (i + 1) % n) for i in range(n)])
    other = lax.ppermute(stash, "dp", [(i, (i + 2 * (i % 2)) % n) for i in range(n)])
    cot_other = hop(grad_out, dh=1)
    weight, down = local(
        pack_body, [shape(2 * FF, width, BF), shape(FF, width, BF)], gate_weight, up_weight, down_weight
    )

    def part(block, after):
        return local(sums_body, [shape(block.shape[0], 2 * FF, F32)], block, weight, after=(after,))[0]

    def cot_part(block, after):
        return local(sums_body, [shape(block.shape[0], FF, F32)], block, down, after=(after,))[0]

    def split(gu, gh, *after):
        tokens = sum(p.shape[0] for p in gu) // 2
        return local(
            functools.partial(split_body, [p.shape[0] for p in gu]),
            [shape(tokens, n * FF, F32) for n in (3, 1, 1, 1)], *gu, *gh, flag=core, after=after,
        )

    def chip_sum(keep, *sends):
        rows = keep.shape[0]
        outs = [shape(rows, 3 * FF, F32), shape(rows, 3 * FF, BF)]
        return local(add_body, outs, keep, *[swap_core(b) for b in sends])

    def acts_of(chip, recv, *after):
        return local(act_body, [shape(chip.shape[0], 3 * FF, BF)], chip, recv, after=after)[0]

    def order(acts, theirs, nz, with_x, *after):
        out = local(
            functools.partial(order_body, nz, with_x),
            [shape(NX * 2 * TOK, 2 * FF, BF)] * nz
            + [shape(nz * 2 * TOK, FF, BF)] * NX
            + [shape(nz * 2 * TOK, 2 * FF, BF)] * (NX if with_x else 0),
            acts, theirs, flag=core, after=after,
        )
        out = list(out)
        return out[:nz], out[nz : nz + NX], out[nz + NX :]

    def project(blocks, full):
        rows, n = blocks[0].shape[0], len(blocks)
        outs = [shape(rows, width, F32 if i in full else BF) for i in range(n)]
        return local(functools.partial(back_body, n), outs, *blocks, weight)

    def fold(own, recv, *after):
        rows = own.shape[0] // 2
        outs = [shape(rows, width, F32), shape(rows, width, BF)]
        return local(fold_body, outs, own, *recv, after=after)

    def join(keep, recv, kinds, *after):
        return local(join_body, [shape(TOK, width, k) for k in kinds], keep, recv, after=after)

    pair, cot = local(
        pair_body, [shape(2 * TOK, width, BF)] * 2, own, other, grad_out, cot_other, after=(weight, down)
    )
    x1, x2, x3 = hop(pair, dx=1), hop(pair, dx=-1), hop(pair, dx=2)
    cu1, cd1, cu2, cd2 = [hop(cot, dz=o) for o in (1, -1, 2, -2)]
    row = stack(pair, x1, x2, x3)
    u1, d1 = hop(row, dz=1), hop(row, dz=-1)
    near = stack(cot, cu1, cd1, cu2, cd2)
    near_u, near_d = hop(near, dx=1), hop(near, dx=-1)
    cd3 = hop(cd2, dz=-1)
    (u1, d1, near_u, near_d, cu2, cd3), _ = tie([u1, d1, near_u, near_d, cu2, cd3], near)
    cu3 = hop(cu2, dz=1)
    u2, d2 = hop(u1, dz=1), hop(d1, dz=-1)
    near_f, c4 = hop(near_u, dx=1), hop(cd3, dz=-1)
    (u2, d2, near_f, cu3, c4), _ = tie([u2, d2, near_f, cu3, c4])
    far = stack(cu3, cd3, c4)
    u3, d3 = hop(u2, dz=1), hop(d2, dz=-1)
    far_u, far_d = hop(far, dx=1), hop(far, dx=-1)
    in1, cot1 = [row, u1, d1, u2, d2], [near, near_u, near_d, near_f]
    gu1, gh1 = [dot_t(b, weight) for b in in1], [dot_t(b, down) for b in cot1]
    (far_u, far_d), mark = tie([far_u, far_d], gu1[-1], gh1[-1])
    chip1, low1 = chip_sum(*split(gu1, gh1, mark))
    their1 = swap_chip(low1)
    half = row.shape[0] // 2
    lo, hi = local(cut_body, [shape(half, width, BF)] * 2, u3, d3, after=(low1,))
    f_lo, f_hi, far_f = hop(lo, dz=1), hop(hi, dz=-1), hop(far_d, dx=-1)
    gu2 = [part(b, lo) for b in (u3, d3)]
    gh2 = [cot_part(b, lo) for b in (far, far_u, far_d)]
    (f_lo, f_hi, far_f), mark = tie([f_lo, f_hi, far_f], *gu2, *gh2)
    in2, cot2 = [u3, d3, f_lo, f_hi], [far, far_u, far_d, far_f]
    gu2 += [part(b, mark) for b in (f_lo, f_hi)]
    chip2, low2 = chip_sum(*split(gu2, gh2 + [cot_part(far_f, mark)]))
    their2 = swap_chip(low2)
    acts1 = acts_of(chip1, their1, low2)

    by_z1, hid1, _ = order(acts1, swap_core(acts1), len(GROUPS[0]), False)
    mine1, one_d, one_u, two_d, two_u = project(by_z1, (0, 1, 2))
    two_d, two_u = hop(two_d, dz=-1), hop(two_u, dz=1)
    acts2 = acts_of(chip2, their2, mine1)
    by_z2, hid2, by_x2 = order(acts2, swap_core(acts2), len(GROUPS[1]), True)
    rows2, half2 = by_x2[0].shape[0], width // 2
    mine2, *out2, right_keep, right_send = local(
        cross_body,
        [shape(rows2, half2, F32)] + [shape(rows2, half2, BF)] * 3
        + [shape(2 * rows2, half2, F32), shape(2 * rows2, half2, BF)],
        *by_x2, weight,
    )
    right_recv = hop(right_send, dh=1)
    recv2 = [hop(out2[i - 1], dx=X_OFF[i]) for i in (1, 2, 3)]
    one_d, one_u = local(
        carry_body, [shape(8 * TOK, width, BF)] * 2, one_d, two_d, one_u, two_u, after=(mine2,)
    )
    recv1 = [hop(one_d, dz=-1), hop(one_u, dz=1)]
    far_row = stack(f_lo, f_hi, after=(one_d,))
    grad_gate, grad_up, mark_a = weight_grad(by_z1 + by_z2, in1 + [u3, d3, far_row], (0, FF), ff)
    keep2, send2 = local(
        fold_body, [shape(rows2 // 2, half2, F32), shape(rows2 // 2, half2, BF)],
        mine2, *recv2, after=(mark_a,),
    )
    right_own, *right_out = local(
        join_body, [shape(rows2 // 2, half2, F32)] + [shape(rows2 // 2, half2, BF)] * 3,
        right_keep, right_recv, after=(pause(2_400_000_000, keep2),),
    )
    right_in = [hop(right_out[i - 1], dx=X_OFF[i]) for i in (3, 1, 2)]
    recv2 = hop(send2, dh=1)
    grad_down, mark_b = weight_grad(hid1 + hid2, cot1 + cot2, (0,), ff, right_own)
    out2 = local(
        merge_body, [shape(TOK, width, BF)] * 3, keep2, recv2, right_own, *right_in, after=(mark_b,)
    )
    sent = [hop(b, dz=Z_OFF[z]) for z, b in zip(GROUPS[1], out2)]
    keep1, send1 = fold(mine1, recv1, pause(1_200_000_000, out2[0]))
    own_sum, *out1 = join(keep1, hop(send1, dh=1), [F32] + [BF] * 3, pause(2_300_000_000, out2[0]))
    sent += [hop(out1[i - 1], dx=X_OFF[i]) for i in (3, 1, 2)]
    (grad_input,) = local(last_body, [shape(TOK, width, BF)], own_sum, *sent)
    return grad_input, grad_gate, grad_up, grad_down


def solution(mesh):
    spec = P("dp", "seq")
    return jax.shard_map(
        per_device, mesh=mesh, in_specs=(spec,) * 5, out_specs=(spec,) * 4, check_vma=False
    )
```

```python
import functools

import jax
import jax.numpy as jnp
from jax import lax
from jax.experimental import pallas as pl
from jax.experimental.pallas import tpu as pltpu
from jax.sharding import PartitionSpec as P

NX, NZ, NH = 4, 8, 2
BF, F32 = jnp.bfloat16, jnp.float32
Z_OFF = (0, -1, 1, -2, 2, -3, 3, 4)
X_OFF = (0, -1, 1, 2)
GROUPS = ((0, 1, 2, 3, 4), (5, 6, 7))
TOK = 16
FF = 256
LIMIT = 16 * 2**20
SMALL = pl.CostEstimate(flops=1, bytes_accessed=1, transcendentals=0)


def dp_index(x, z, h):
    return ((x % NX) * NZ + z % NZ) * NH + h % NH


def hop(block, dx=0, dz=0, dh=0):
    route = [
        (dp_index(x, z, h), dp_index(x + dx, z + dz, h + dh))
        for x in range(NX)
        for z in range(NZ)
        for h in range(NH)
    ]
    return lax.ppermute(block, "dp", route)


def swap_core(block):
    return lax.ppermute(block, "seq", [(0, 1), (1, 0), (2, 3), (3, 2)])


def swap_chip(block):
    return lax.ppermute(block, "seq", [(0, 2), (2, 0), (1, 3), (3, 1)])


def dot_t(left, right):
    return lax.dot_general(left, right, (((1,), (1,)), ((), ())), preferred_element_type=F32)


def dot_first(left, right):
    return lax.dot_general(left, right, (((0,), (0,)), ((), ())), preferred_element_type=F32)


def local(body, outs, *args, flag=None, after=(), cost=SMALL):
    n, first = len(args), 0 if flag is None else 1

    def run(*refs):
        body(*refs[: n + first], *refs[n + first + len(after) :])

    vmem, free = pl.BlockSpec(memory_space=pltpu.VMEM), pl.BlockSpec(memory_space=pl.ANY)
    return pl.pallas_call(
        run,
        out_shape=list(outs),
        in_specs=[pl.BlockSpec(memory_space=pltpu.SMEM)] * first + [vmem] * n + [free] * len(after),
        out_specs=[vmem] * len(outs),
        compiler_params=pltpu.CompilerParams(vmem_limit_bytes=LIMIT),
        cost_estimate=cost,
    )(*([] if flag is None else [flag]), *args, *after)


def shape(rows, cols, kind):
    return jax.ShapeDtypeStruct((rows, cols), kind)


def stack_body(*refs):
    out, at = refs[-1], 0
    for ref in refs[:-1]:
        rows = ref.shape[0]
        out[at : at + rows] = ref[...]
        at += rows


def stack(*blocks, after=()):
    rows = sum(b.shape[0] for b in blocks)
    out = shape(rows, blocks[0].shape[1], blocks[0].dtype)
    return local(stack_body, [out], *blocks, after=after)[0]


def sums_body(block, weight, out):
    out[...] = dot_t(block[...], weight[...])


def cut_body(a, b, lo, hi):
    half = lo.shape[0]
    lo[...] = a[:half]
    hi[...] = b[half:]


def split_body(rows_in, flag, *refs):
    n = len(rows_in)
    gus, ghs, (keep, send_g, send_u, send_h) = refs[:n], refs[n:-4], refs[-4:]
    first = flag[0] == 0
    at = 0
    for ref, rows in zip(gus, rows_in):
        for i in range(rows // (2 * TOK)):
            a = ref[2 * TOK * i : 2 * TOK * i + TOK]
            b = ref[2 * TOK * i + TOK : 2 * TOK * (i + 1)]
            keep[at : at + TOK, : 2 * FF] = jnp.where(first, a, b)
            send = jnp.where(first, b, a)
            send_g[at : at + TOK], send_u[at : at + TOK] = send[:, :FF], send[:, FF:]
            at += TOK
    for x, ref in enumerate(ghs):
        for i in range(ref.shape[0] // (2 * TOK)):
            a = ref[2 * TOK * i : 2 * TOK * i + TOK]
            b = ref[2 * TOK * i + TOK : 2 * TOK * (i + 1)]
            at = (i * NX + x) * TOK
            keep[at : at + TOK, 2 * FF :] = jnp.where(first, a, b)
            send_h[at : at + TOK] = jnp.where(first, b, a)


def add_body(a, g, u, h, full, low):
    for lo, b in ((0, g), (FF, u), (2 * FF, h)):
        hi = lo + FF
        total = a[:, lo:hi] + b[...]
        full[:, lo:hi] = total
        low[:, lo:hi] = total.astype(BF)


def act_body(a, b, out):
    gate = a[:, :FF] + b[:, :FF].astype(F32)
    up = a[:, FF : 2 * FF] + b[:, FF : 2 * FF].astype(F32)
    grad_hidden = a[:, 2 * FF :] + b[:, 2 * FF :].astype(F32)
    sig = 1.0 / (1.0 + jnp.exp(-gate))
    act = gate * sig
    out[:, :FF] = (act * up).astype(BF)
    out[:, FF : 2 * FF] = (grad_hidden * up * sig * (1.0 + gate * (1.0 - sig))).astype(BF)
    out[:, 2 * FF :] = (grad_hidden * act).astype(BF)


def order_body(nz, with_x, flag, mine, theirs, *outs):
    by_z, hid, by_x = outs[:nz], outs[nz : nz + NX], outs[nz + NX :]
    first = flag[0] == 0
    for z in range(nz):
        for x in range(NX):
            at = (z * NX + x) * TOK
            a, b = mine[at : at + TOK], theirs[at : at + TOK]
            for h, val in enumerate((jnp.where(first, a, b), jnp.where(first, b, a))):
                to = (2 * z + h) * TOK
                hid[x][to : to + TOK] = val[:, :FF]
                if with_x:
                    by_x[x][to : to + TOK] = val[:, FF:]
                to = (2 * x + h) * TOK
                by_z[z][to : to + TOK] = val[:, FF:]


def fold_body(own, *refs):
    parts, outs = refs[:-2], refs[-2:]
    for i in range(outs[0].shape[0] // TOK):
        for h, out in enumerate(outs):
            s = slice((2 * i + h) * TOK, (2 * i + h + 1) * TOK)
            total = own[s]
            for part in parts:
                total = total + part[s].astype(F32)
            out[i * TOK : (i + 1) * TOK] = total.astype(out.dtype)


def cross_body(*refs):
    blocks, weight, lefts, (keep, send) = refs[:NX], refs[NX], refs[NX + 1 : -2], refs[-2:]
    half, rows = weight.shape[1] // 2, keep.shape[0] // NX

    @pl.loop(0, half // 512)
    def _(j):
        cols = pl.ds(pl.multiple_of(j * 512, 512), 512)
        right = pl.ds(pl.multiple_of(half + j * 512, 512), 512)
        for x, (block, out) in enumerate(zip(blocks, lefts)):
            part = jnp.dot(block[...], weight[:, cols], preferred_element_type=F32)
            out[:, cols] = part.astype(out.dtype)
            part = jnp.dot(block[...], weight[:, right], preferred_element_type=F32)
            for i in range(rows // TOK):
                to = x * rows + i * TOK
                keep[to : to + TOK, cols] = part[2 * i * TOK : (2 * i + 1) * TOK]
                send[to : to + TOK, cols] = part[(2 * i + 1) * TOK : (2 * i + 2) * TOK].astype(BF)


def merge_body(keep, recv, own, a, b, c, *outs):
    half = keep.shape[1]
    for i, out in enumerate(outs):
        s = slice(i * TOK, (i + 1) * TOK)
        out[:, :half] = (keep[s] + recv[s].astype(F32)).astype(BF)
        total = own[s] + a[s].astype(F32) + b[s].astype(F32) + c[s].astype(F32)
        out[:, half:] = total.astype(BF)


def carry_body(a, b, c, d, lo, hi):
    lo[...] = (a[...] + b[...].astype(F32)).astype(BF)
    hi[...] = (c[...] + d[...].astype(F32)).astype(BF)


def join_body(keep, recv, *outs):
    for i, out in enumerate(outs):
        rows = out.shape[0]
        s = slice(i * rows, (i + 1) * rows)
        out[...] = (keep[s] + recv[s].astype(F32)).astype(out.dtype)


def last_body(own, *refs):
    parts, out = refs[:-1], refs[-1]
    total = own[...]
    for part in parts:
        total = total + part[...].astype(F32)
    out[...] = total.astype(BF)


def weight_grad_body(n, m, los, refs_after, *refs):
    acts, blocks, rest = refs[:n], refs[n : n + m], refs[n + m + refs_after :]
    outs, mark, held, sems = rest[: len(los)], rest[len(los)], rest[len(los) + 1 : -1], rest[-1]
    mark[...] = jnp.zeros_like(mark)
    left = [jnp.concatenate([a[:, lo : lo + FF] for a in acts]) for lo in los]
    copies, tile = [], 1024
    for j in range(held[0].shape[1] // tile):
        cols = slice(j * tile, (j + 1) * tile)
        right = jnp.concatenate([b[:, cols] for b in blocks])
        for i, (lhs, out, buf) in enumerate(zip(left, outs, held)):
            buf[:, cols] = dot_first(lhs, right)[: buf.shape[0]]
            copies.append(pltpu.make_async_copy(buf.at[:, cols], out.at[:, cols], sems.at[i, j]))
            copies[-1].start()
    for copy in copies:
        copy.wait()


def weight_grad(acts, blocks, los, ff, *after):
    vmem, free = pl.BlockSpec(memory_space=pltpu.VMEM), pl.BlockSpec(memory_space=pl.ANY)
    n, m, width = len(acts), len(blocks), blocks[0].shape[1]
    return pl.pallas_call(
        functools.partial(weight_grad_body, n, m, los, len(after)),
        out_shape=[shape(ff, width, F32)] * len(los) + [shape(8, 128, F32)],
        in_specs=[vmem] * (n + m) + [free] * len(after),
        out_specs=[free] * len(los) + [vmem],
        scratch_shapes=[pltpu.VMEM((ff, width), F32)] * len(los)
        + [pltpu.SemaphoreType.DMA((len(los), width // 1024))],
        compiler_params=pltpu.CompilerParams(vmem_limit_bytes=LIMIT),
        cost_estimate=SMALL,
    )(*acts, *blocks, *after)


def tie_body(n, *refs):
    refs[-1][...] = jnp.zeros_like(refs[-1])


def tie(values, *after):
    n = len(values)
    *out, mark = pl.pallas_call(
        functools.partial(tie_body, n),
        out_shape=[jax.ShapeDtypeStruct(v.shape, v.dtype) for v in values] + [shape(8, 128, F32)],
        in_specs=[pl.BlockSpec(memory_space=pl.ANY)] * (n + len(after)),
        out_specs=[pl.BlockSpec(memory_space=pl.ANY)] * n + [pl.BlockSpec(memory_space=pltpu.VMEM)],
        input_output_aliases={i: i for i in range(n)},
        compiler_params=pltpu.CompilerParams(vmem_limit_bytes=2**20),
        cost_estimate=SMALL,
    )(*values, *after)
    return out, mark


def pause(flops, after):
    return pl.pallas_call(
        functools.partial(tie_body, 0),
        out_shape=shape(8, 128, F32),
        in_specs=[pl.BlockSpec(memory_space=pl.ANY)],
        out_specs=pl.BlockSpec(memory_space=pltpu.VMEM),
        compiler_params=pltpu.CompilerParams(vmem_limit_bytes=2**20),
        cost_estimate=pl.CostEstimate(flops=flops, bytes_accessed=1, transcendentals=0),
    )(after)


def pack_body(gate, up, down, weight, down_out):
    ff, width = gate.shape
    pad = jnp.zeros((FF - ff, width), BF)
    weight[:ff] = gate[...]
    weight[ff:FF] = pad
    weight[FF : FF + ff] = up[...]
    weight[FF + ff :] = pad
    down_out[:ff] = down[...]
    down_out[ff:] = pad


def pair_body(own, other, cot_own, cot_other, pair, cot):
    pair[:TOK] = own[...]
    pair[TOK:] = other[...]
    cot[:TOK] = cot_own[...]
    cot[TOK:] = cot_other[...]


def back_body(n, *refs):
    blocks, weight, outs = refs[:n], refs[n], refs[n + 1 :]

    @pl.loop(0, weight.shape[1] // 512)
    def _(j):
        cols = pl.ds(pl.multiple_of(j * 512, 512), 512)
        for block, out in zip(blocks, outs):
            part = jnp.dot(block[...], weight[:, cols], preferred_element_type=F32)
            out[:, cols] = part.astype(out.dtype)


def per_device(stash, grad_out, gate_weight, up_weight, down_weight):
    core = (lax.axis_index("seq") % 2).astype(jnp.int32).reshape(1)
    ff, width = gate_weight.shape
    n = NX * NZ * NH
    own = lax.ppermute(stash, "dp", [(i, (i + 1) % n) for i in range(n)])
    other = lax.ppermute(stash, "dp", [(i, (i + 2 * (i % 2)) % n) for i in range(n)])
    cot_other = hop(grad_out, dh=1)
    weight, down = local(
        pack_body, [shape(2 * FF, width, BF), shape(FF, width, BF)], gate_weight, up_weight, down_weight
    )

    def part(block, after):
        return local(sums_body, [shape(block.shape[0], 2 * FF, F32)], block, weight, after=(after,))[0]

    def cot_part(block, after):
        return local(sums_body, [shape(block.shape[0], FF, F32)], block, down, after=(after,))[0]

    def split(gu, gh, *after):
        tokens = sum(p.shape[0] for p in gu) // 2
        return local(
            functools.partial(split_body, [p.shape[0] for p in gu]),
            [shape(tokens, n * FF, F32) for n in (3, 1, 1, 1)], *gu, *gh, flag=core, after=after,
        )

    def chip_sum(keep, *sends):
        rows = keep.shape[0]
        outs = [shape(rows, 3 * FF, F32), shape(rows, 3 * FF, BF)]
        return local(add_body, outs, keep, *[swap_core(b) for b in sends])

    def acts_of(chip, recv, *after):
        return local(act_body, [shape(chip.shape[0], 3 * FF, BF)], chip, recv, after=after)[0]

    def order(acts, theirs, nz, with_x, *after):
        out = local(
            functools.partial(order_body, nz, with_x),
            [shape(NX * 2 * TOK, 2 * FF, BF)] * nz
            + [shape(nz * 2 * TOK, FF, BF)] * NX
            + [shape(nz * 2 * TOK, 2 * FF, BF)] * (NX if with_x else 0),
            acts, theirs, flag=core, after=after,
        )
        out = list(out)
        return out[:nz], out[nz : nz + NX], out[nz + NX :]

    def project(blocks, full):
        rows, n = blocks[0].shape[0], len(blocks)
        outs = [shape(rows, width, F32 if i in full else BF) for i in range(n)]
        return local(functools.partial(back_body, n), outs, *blocks, weight)

    def fold(own, recv, *after):
        rows = own.shape[0] // 2
        outs = [shape(rows, width, F32), shape(rows, width, BF)]
        return local(fold_body, outs, own, *recv, after=after)

    def join(keep, recv, kinds, *after):
        return local(join_body, [shape(TOK, width, k) for k in kinds], keep, recv, after=after)

    pair, cot = local(
        pair_body, [shape(2 * TOK, width, BF)] * 2, own, other, grad_out, cot_other, after=(weight, down)
    )
    x1, x2, x3 = hop(pair, dx=1), hop(pair, dx=-1), hop(pair, dx=2)
    cu1, cd1, cu2, cd2 = [hop(cot, dz=o) for o in (1, -1, 2, -2)]
    row = stack(pair, x1, x2, x3)
    u1, d1 = hop(row, dz=1), hop(row, dz=-1)
    near = stack(cot, cu1, cd1, cu2, cd2)
    near_u, near_d = hop(near, dx=1), hop(near, dx=-1)
    cd3 = hop(cd2, dz=-1)
    (u1, d1, near_u, near_d, cu2, cd3), _ = tie([u1, d1, near_u, near_d, cu2, cd3], near)
    cu3 = hop(cu2, dz=1)
    u2, d2 = hop(u1, dz=1), hop(d1, dz=-1)
    near_f, c4 = hop(near_u, dx=1), hop(cd3, dz=-1)
    (u2, d2, near_f, cu3, c4), _ = tie([u2, d2, near_f, cu3, c4])
    far = stack(cu3, cd3, c4)
    u3, d3 = hop(u2, dz=1), hop(d2, dz=-1)
    far_u, far_d = hop(far, dx=1), hop(far, dx=-1)
    in1, cot1 = [row, u1, d1, u2, d2], [near, near_u, near_d, near_f]
    gu1, gh1 = [dot_t(b, weight) for b in in1], [dot_t(b, down) for b in cot1]
    (far_u, far_d), mark = tie([far_u, far_d], gu1[-1], gh1[-1])
    chip1, low1 = chip_sum(*split(gu1, gh1, mark))
    their1 = swap_chip(low1)
    half = row.shape[0] // 2
    lo, hi = local(cut_body, [shape(half, width, BF)] * 2, u3, d3, after=(low1,))
    f_lo, f_hi, far_f = hop(lo, dz=1), hop(hi, dz=-1), hop(far_d, dx=-1)
    gu2 = [part(b, lo) for b in (u3, d3)]
    gh2 = [cot_part(b, lo) for b in (far, far_u, far_d)]
    (f_lo, f_hi, far_f), mark = tie([f_lo, f_hi, far_f], *gu2, *gh2)
    in2, cot2 = [u3, d3, f_lo, f_hi], [far, far_u, far_d, far_f]
    gu2 += [part(b, mark) for b in (f_lo, f_hi)]
    chip2, low2 = chip_sum(*split(gu2, gh2 + [cot_part(far_f, mark)]))
    their2 = swap_chip(low2)
    acts1 = acts_of(chip1, their1, low2)

    by_z1, hid1, _ = order(acts1, swap_core(acts1), len(GROUPS[0]), False)
    mine1, one_d, one_u, two_d, two_u = project(by_z1, (0, 1, 2))
    two_d, two_u = hop(two_d, dz=-1), hop(two_u, dz=1)
    acts2 = acts_of(chip2, their2, mine1)
    by_z2, hid2, by_x2 = order(acts2, swap_core(acts2), len(GROUPS[1]), True)
    rows2, half2 = by_x2[0].shape[0], width // 2
    mine2, *out2, right_keep, right_send = local(
        cross_body,
        [shape(rows2, half2, F32)] + [shape(rows2, half2, BF)] * 3
        + [shape(2 * rows2, half2, F32), shape(2 * rows2, half2, BF)],
        *by_x2, weight,
    )
    right_recv = hop(right_send, dh=1)
    recv2 = [hop(out2[i - 1], dx=X_OFF[i]) for i in (1, 2, 3)]
    one_d, one_u = local(
        carry_body, [shape(8 * TOK, width, BF)] * 2, one_d, two_d, one_u, two_u, after=(mine2,)
    )
    recv1 = [hop(one_d, dz=-1), hop(one_u, dz=1)]
    grad_gate, grad_up, mark_a = weight_grad(by_z1 + by_z2, in1 + in2, (0, FF), ff, one_d)
    keep2, send2 = local(
        fold_body, [shape(rows2 // 2, half2, F32), shape(rows2 // 2, half2, BF)],
        mine2, *recv2, after=(mark_a,),
    )
    right_own, *right_out = local(
        join_body, [shape(rows2 // 2, half2, F32)] + [shape(rows2 // 2, half2, BF)] * 3,
        right_keep, right_recv, after=(pause(2_400_000_000, keep2),),
    )
    right_in = [hop(right_out[i - 1], dx=X_OFF[i]) for i in (3, 1, 2)]
    recv2 = hop(send2, dh=1)
    grad_down, mark_b = weight_grad(hid1 + hid2, cot1 + cot2, (0,), ff, right_own)
    out2 = local(
        merge_body, [shape(TOK, width, BF)] * 3, keep2, recv2, right_own, *right_in, after=(mark_b,)
    )
    sent = [hop(b, dz=Z_OFF[z]) for z, b in zip(GROUPS[1], out2)]
    keep1, send1 = fold(mine1, recv1, pause(1_200_000_000, out2[0]))
    own_sum, *out1 = join(keep1, hop(send1, dh=1), [F32] + [BF] * 3, pause(2_300_000_000, out2[0]))
    sent += [hop(out1[i - 1], dx=X_OFF[i]) for i in (3, 1, 2)]
    (grad_input,) = local(last_body, [shape(TOK, width, BF)], own_sum, *sent)
    return grad_input, grad_gate, grad_up, grad_down


def solution(mesh):
    spec = P("dp", "seq")
    return jax.shard_map(
        per_device, mesh=mesh, in_specs=(spec,) * 5, out_specs=(spec,) * 4, check_vma=False
    )
```
